32 devices in a mesh: rows: 4 (over z), lag: 8 (over y, x, core).
Axes of the slice: x: 2, y: 2, z: 4, core: 2. Of those that a mesh axis runs over, the one named last changes fastest.
Arguments:
- excitation: bfloat16 [4, 2048, 128], P(None, 'rows'), may hold values from -6 to 6
- pending: float32 [8, 2048, 128], P('lag', 'rows'), may hold values from -6 to 6
- inverse: float32 [16, 128, 128], P('rows'), may hold values from -0.5 to 0.5
- interaction: bfloat16 [3072, 128, 128], P(('rows', 'lag')), may hold values from -0.0390625 to 0.0390625
- slot_row: int32 [3072], P(('rows', 'lag')), may hold values from 0 to 3
- slot_owner: int32 [3072], P(('rows', 'lag')), may hold values from 0 to 3
- slot_pos: int32 [3072], P(('rows', 'lag')), may hold values from 0 to 1
- needed: int32 [32, 4, 2], P(('rows', 'lag')), may hold values from 0 to 3
- block_count: int32 [4, 8], P('rows', 'lag'), may hold values from 6 to 96, as said below
Outputs:
- currents: bfloat16 [4, 2048, 128], P(None, 'rows')
- carried: float32 [8, 2048, 128], P('lag', 'rows')
The draws below stay inside these ranges and needn't reach their ends.
Inputs may be any that keep to these rules, and one draw needn't show every extreme that they name: `block_count`: every row owner and lag has at least 6 live slots, and some row owner and lag has all 96 live.
All inputs are finite; a program needn't handle non-finite values.
Results may differ from the reference program's by a relative error of at most 0.002.
Values may be sent and summed in bfloat16 or wider, within the bound.
A program may use at most 64 MiB of HBM per device.

```python
import jax
import jax.numpy as jnp
from jax import lax

BLK = 128
EXC = 128
STEPS = 4
RB_DEV = 4
BPR = 24
K_DEV = 96
CAP = 2
ROW_BLOCKS = 16
UNKNOWNS = 2048
N_ROWS = 4
N_LAG = 8


def draw_block_count(key, part):
    first_key = jax.random.fold_in(key, 11)
    second_key = jax.random.fold_in(key, 23)
    uniform_count = jax.random.randint(first_key, (N_ROWS * N_LAG,), 0, K_DEV + 1)
    counted = jnp.maximum(K_DEV // 16, uniform_count * uniform_count // K_DEV)
    chosen = jax.random.randint(second_key, (), 0, N_ROWS * N_LAG)
    counted = jnp.where(jnp.arange(N_ROWS * N_LAG) == chosen, K_DEV, counted)
    return counted.reshape(N_ROWS, N_LAG).astype(jnp.int32)


def touch_ends(result, key, least, top_value):
    place = [jax.random.randint(jax.random.fold_in(key, axis), (), 0, length) for axis, length in enumerate(result.shape)]
    longest = result.shape.index(max(result.shape))
    beside = place[:longest] + [(place[longest] + 1) % result.shape[longest]] + place[longest + 1:]
    return result.at[tuple(place)].set(least).at[tuple(beside)].set(top_value)


def shard_levels(rng, extent, cuts, smallest, largest):
    gain, own = 1.0, jax.random.fold_in(rng, 6)
    for axis_at, blocks in cuts:
        draws = jnp.exp(jax.random.uniform(jax.random.fold_in(own, axis_at), (blocks,), jnp.float32, smallest / len(cuts), largest / len(cuts)))
        gain = gain * jnp.repeat(draws, extent[axis_at] // blocks).reshape([-1 if axis == axis_at else 1 for axis in range(len(extent))])
    return gain


def centred(own_key, shape, deviation, limit, pieces=(), kind=jnp.bfloat16):
    drawn = jax.random.normal(own_key, shape, jnp.float32) * deviation
    if len(pieces) > 0:
        drawn = shard_levels(own_key, shape, pieces, -0.22, 0.18) * drawn
    return jnp.clip(drawn, min=-limit, max=limit).astype(kind)


def setup_inputs(seed: int = 0) -> dict:
    seeds = jax.random.split(jax.random.key(seed), 10)
    return {
        "excitation": centred(seeds[0], (STEPS, UNKNOWNS, EXC), 1.0, 6.0, ((1, 4),)),
        "pending": centred(seeds[1], (N_LAG, UNKNOWNS, EXC), 1.0, 6.0, ((0, 8), (1, 4)), jnp.float32),
        "inverse": centred(seeds[2], (ROW_BLOCKS, BLK, BLK), BLK ** -0.5, 0.5, ((0, 4),), jnp.float32),
        "interaction": centred(seeds[3], (N_ROWS * N_LAG * K_DEV, BLK, BLK), (BLK * BPR * N_LAG) ** -0.5, 0.0390625, ((0, 32),)),
        "slot_row": touch_ends(jax.random.randint(seeds[4], (N_ROWS * N_LAG * K_DEV,), 0, RB_DEV), jax.random.fold_in(seeds[4], 1), 0, RB_DEV - 1).astype(jnp.int32),
        "slot_owner": touch_ends(jax.random.randint(seeds[5], (N_ROWS * N_LAG * K_DEV,), 0, N_ROWS), jax.random.fold_in(seeds[5], 1), 0, N_ROWS - 1).astype(jnp.int32),
        "slot_pos": touch_ends(jax.random.randint(seeds[6], (N_ROWS * N_LAG * K_DEV,), 0, CAP), jax.random.fold_in(seeds[6], 1), 0, CAP - 1).astype(jnp.int32),
        "needed": touch_ends(jax.random.randint(seeds[7], (N_ROWS * N_LAG, N_ROWS, CAP), 0, RB_DEV), jax.random.fold_in(seeds[7], 1), 0, RB_DEV - 1).astype(jnp.int32),
        "block_count": draw_block_count(jax.random.fold_in(seeds[9], 71), 0),
    }


def lag_terms(solved, interaction, slot_row, slot_owner, slot_pos, needed, block_count):
    blocks = solved.reshape(ROW_BLOCKS, BLK, EXC).astype(jnp.float32)
    inter_all = interaction.reshape(N_ROWS * N_LAG, K_DEV, BLK, BLK)
    rows_all = slot_row.reshape(N_ROWS * N_LAG, K_DEV)
    owner_all = slot_owner.reshape(N_ROWS * N_LAG, K_DEV)
    pos_all = slot_pos.reshape(N_ROWS * N_LAG, K_DEV)
    need_all = needed.reshape(N_ROWS * N_LAG, N_ROWS, CAP)
    count_all = block_count.reshape(N_ROWS * N_LAG)

    def lag_block(flat_index):
        need_table = need_all[flat_index]
        owners = owner_all[flat_index]
        local_block = need_table[owners, pos_all[flat_index]]
        column = (owners * RB_DEV + local_block).astype(jnp.int32)
        picked = blocks[column]
        products = jnp.einsum("kij,kje->kie", inter_all[flat_index].astype(jnp.float32), picked,
                              precision=lax.Precision.HIGHEST)
        live_slots = jnp.arange(K_DEV, dtype=jnp.int32) < count_all[flat_index]
        placing = ((rows_all[flat_index][None, :] == jnp.arange(RB_DEV, dtype=jnp.int32)[:, None])
                   & live_slots[None, :]).astype(jnp.float32)
        return jnp.einsum("bk,kie->bie", placing, products, precision=lax.Precision.HIGHEST)

    results = lax.map(lag_block, jnp.arange(N_ROWS * N_LAG, dtype=jnp.int32))
    results = results.reshape(N_ROWS, N_LAG, RB_DEV * BLK, EXC)
    return jnp.transpose(results, (1, 0, 2, 3)).reshape(N_LAG, UNKNOWNS, EXC)


def reference(excitation, pending, inverse, interaction, slot_row, slot_owner, slot_pos, needed, block_count):
    accumulated = pending
    outputs = []
    for step_index in range(STEPS):
        right_side = excitation[step_index].astype(jnp.float32) - accumulated[0]
        solved = jnp.einsum("bij,bje->bie", inverse, right_side.reshape(ROW_BLOCKS, BLK, EXC),
                            precision=lax.Precision.HIGHEST)
        solved = solved.reshape(UNKNOWNS, EXC).astype(jnp.bfloat16)
        outputs.append(solved)
        terms = lag_terms(solved, interaction, slot_row, slot_owner, slot_pos, needed, block_count)
        shifted = jnp.concatenate([accumulated[1:], jnp.zeros((1, UNKNOWNS, EXC), jnp.float32)], axis=0)
        accumulated = shifted + terms
    return jnp.stack(outputs), accumulated
```

```python
import functools

import jax
import jax.numpy as jnp
from jax import lax
from jax.experimental import pallas as pl
from jax.experimental.pallas import tpu as pltpu
from jax.sharding import PartitionSpec as P

MESH = pl.DeviceIdType.MESH


def collapse_kernel(chunk, row_ref, owner_ref, pos_ref, count_ref, block_ref, high_ref, low_ref, total):
    row_blocks, columns, block_size, _ = total.shape
    capacity = count_ref[1]
    first = pl.program_id(0) * chunk

    @pl.when(pl.program_id(0) == 0)
    def _():
        total[...] = jnp.zeros_like(total)

    def add_slot(index, carry):
        slot = first + index
        row = row_ref[slot]
        column = owner_ref[slot] * capacity + pos_ref[slot]
        total[row, column] += block_ref[index].astype(jnp.float32)
        return carry

    live = jnp.clip(count_ref[0] - first, 0, chunk)
    lax.fori_loop(0, live, add_slot, 0)

    @pl.when(pl.program_id(0) == pl.num_programs(0) - 1)
    def _():
        for row in range(row_blocks):
            for column in range(columns):
                value = total[row, column]
                high = value.astype(jnp.bfloat16)
                low = (value - high.astype(jnp.float32)).astype(jnp.bfloat16)
                place = (pl.ds(row * block_size, block_size), pl.ds(column * block_size, block_size))
                high_ref[place] = high
                low_ref[place] = low


def collapse(interaction, slot_row, slot_owner, slot_pos, block_count, row_blocks, columns, capacity):
    slots, block_size, _ = interaction.shape
    chunk = max(size for size in range(1, 17) if slots % size == 0)
    count = jnp.stack([block_count[0, 0], jnp.int32(capacity)])
    shape = (row_blocks * block_size, columns * block_size)
    whole = pl.BlockSpec(shape, lambda step, *_: (0, 0))
    return pl.pallas_call(
        functools.partial(collapse_kernel, chunk),
        grid_spec=pltpu.PrefetchScalarGridSpec(
            num_scalar_prefetch=4,
            grid=(slots // chunk,),
            in_specs=[pl.BlockSpec((chunk, block_size, block_size), lambda step, *_: (step, 0, 0))],
            out_specs=[whole, whole],
            scratch_shapes=[pltpu.VMEM((row_blocks, columns, block_size, block_size), jnp.float32)],
        ),
        out_shape=[jax.ShapeDtypeStruct(shape, jnp.bfloat16)] * 2,
        compiler_params=pltpu.CompilerParams(vmem_limit_bytes=40 * 1024 * 1024),
    )(slot_row, slot_owner, slot_pos, count, interaction)


def window_kernel(
    rows, lags, steps, row_blocks, capacity,
    excitation, pending, inverse, table, needed, high_hbm, low_hbm,
    currents, carried,
    high, low, own, sending, landed, handed, summed, asked, asked_scalar,
    row_send, row_recv, lag_send, lag_recv, hand_send, hand_recv, ask_send, ask_recv, local_sem, out_sem,
):
    row = lax.axis_index("rows")
    lag = lax.axis_index("lag")
    block_size = inverse.shape[1]

    barrier = pltpu.get_barrier_semaphore()
    for away in range(1, rows):
        pl.semaphore_signal(barrier, inc=1, device_id=(lax.rem(row + away, rows), lag), device_id_type=MESH)
    for away in range(1, lags):
        pl.semaphore_signal(barrier, inc=1, device_id=(row, lax.rem(lag + away, lags)), device_id_type=MESH)

    fetch_high = pltpu.make_async_copy(high_hbm, high, local_sem.at[0])
    fetch_low = pltpu.make_async_copy(low_hbm, low, local_sem.at[1])
    fetch_high.start()
    fetch_low.start()

    def solve(step):
        for block in range(row_blocks):
            place = pl.ds(block * block_size, block_size)
            before = pending[0, place] if step == 0 else summed[step - 1, place]
            right_side = excitation[step, place].astype(jnp.float32) - before
            solved = jnp.dot(
                inverse[block], right_side, precision=lax.Precision.HIGHEST,
                preferred_element_type=jnp.float32,
            )
            own[step][block] = solved.astype(jnp.bfloat16)

    @pl.when(lag == 0)
    def _():
        solve(0)

    pl.semaphore_wait(barrier, rows + lags - 2)

    def ask_copy(away):
        target = lax.rem(row + away, rows)
        return pltpu.make_async_remote_copy(
            src_ref=table, dst_ref=asked.at[away - 1], send_sem=ask_send.at[away - 1],
            recv_sem=ask_recv.at[away - 1], device_id=(target, lag), device_id_type=MESH,
        )

    def row_copy(step, away):
        target = lax.rem(row + away, rows)
        return pltpu.make_async_remote_copy(
            src_ref=sending.at[step, away - 1], dst_ref=landed.at[step, row],
            send_sem=row_send.at[step, away - 1], recv_sem=row_recv.at[step, away - 1],
            device_id=(target, lag), device_id_type=MESH,
        )

    def lag_copy(step, target, which):
        return pltpu.make_async_remote_copy(
            src_ref=own[step], dst_ref=own[step],
            send_sem=lag_send.at[step, which], recv_sem=lag_recv.at[step],
            device_id=(row, target), device_id_type=MESH,
        )

    def hand_copy(step):
        source = pending.at[0] if step == 0 else summed.at[step - 1]
        return pltpu.make_async_remote_copy(
            src_ref=source, dst_ref=handed.at[step],
            send_sem=hand_send.at[step], recv_sem=hand_recv.at[step],
            device_id=(row, lax.rem(lag + lags - 1, lags)), device_id_type=MESH,
        )

    def out_copy(step):
        return pltpu.make_async_copy(own[step], currents.at[step], out_sem.at[step])

    for away in range(1, rows):
        ask_copy(away).start()

    @pl.when(lag > 0)
    def _():
        hand_copy(0).start()

    to_scalar = pltpu.make_async_copy(asked, asked_scalar, local_sem.at[2])
    evens = list(range(2, lags, 2))
    forwards = (lag > 0) & (lax.rem(lag, 2) == 0) & (lag + 1 < lags)

    for step in range(steps):
        last = step == steps - 1

        @pl.when(lag == 0)
        def _():
            if step > 0:
                solve(step)

        @pl.when(lag > 0)
        def _():
            lag_copy(step, 0, 0).wait_recv()

        if step == 0:
            for away in range(1, rows):
                ask_copy(away).wait_recv()
            to_scalar.start()
            to_scalar.wait()

        @pl.when(forwards)
        def _():
            lag_copy(step, lag + 1, 0).start()

        if last:
            @pl.when(lag == 0)
            def _():
                lag_copy(step, 1, 0).start()
                for place, target in enumerate(evens):
                    lag_copy(step, target, place + 1).start()

        for away in range(1, rows):
            for entry in range(capacity):
                sending[step, away - 1, entry] = own[step][asked_scalar[rows - away - 1, row, entry]]
            row_copy(step, away).start()

        if not last:
            @pl.when(lag == 0)
            def _():
                for place, target in enumerate(evens):
                    lag_copy(step, target, place + 1).start()

        out_copy(step).start()
        for entry in range(capacity):
            landed[step, row, entry] = own[step][needed[row, entry]]

        for away in range(1, rows):
            row_copy(step, away).wait_recv()

        if not last:
            @pl.when(lag == 0)
            def _():
                lag_copy(step, 1, 0).start()

        if step == 0:
            fetch_high.wait()
            fetch_low.wait()

            @pl.when(lag == lags - 1)
            def _():
                handed[...] = jnp.zeros_like(handed)

        values = landed[step].reshape(rows * capacity * block_size, landed.shape[-1])
        product = jnp.dot(high[...], values, preferred_element_type=jnp.float32)
        product += jnp.dot(low[...], values, preferred_element_type=jnp.float32)

        @pl.when(lag < lags - 1)
        def _():
            hand_copy(step).wait_recv()

        summed[step] = handed[step] + product
        if not last:
            @pl.when(lag > 0)
            def _():
                hand_copy(step + 1).start()

    finish = pltpu.make_async_copy(summed.at[steps - 1], carried.at[0], local_sem.at[3])
    finish.start()

    for away in range(1, rows):
        ask_copy(away).wait_send()
    for step in range(steps):
        for away in range(1, rows):
            row_copy(step, away).wait_send()
        out_copy(step).wait()

        @pl.when(lag > 0)
        def _():
            hand_copy(step).wait_send()

        @pl.when(forwards)
        def _():
            lag_copy(step, lag + 1, 0).wait_send()

        @pl.when(lag == 0)
        def _():
            lag_copy(step, 1, 0).wait_send()
            for place, target in enumerate(evens):
                lag_copy(step, target, place + 1).wait_send()

    finish.wait()


def per_device(
    excitation, pending, inverse, interaction, slot_row, slot_owner, slot_pos, needed, block_count
):
    row_blocks, block_size, _ = inverse.shape
    steps, unknowns, width = excitation.shape
    rows, capacity = needed.shape[1:]
    lags = lax.axis_size("lag")
    columns = rows * capacity
    high, low = collapse(
        interaction, slot_row, slot_owner, slot_pos, block_count, row_blocks, columns, capacity
    )
    table = jnp.pad(needed[0], ((0, -rows % 8), (0, -capacity % 128)))
    vmem = pl.BlockSpec(memory_space=pltpu.VMEM)
    smem = pl.BlockSpec(memory_space=pltpu.SMEM)
    hbm = pl.BlockSpec(memory_space=pl.ANY)
    dma = pltpu.SemaphoreType.DMA
    evens = len(range(2, lags, 2))
    return pl.pallas_call(
        functools.partial(window_kernel, rows, lags, steps, row_blocks, capacity),
        out_shape=[
            jax.ShapeDtypeStruct((steps, row_blocks, block_size, width), jnp.bfloat16),
            jax.ShapeDtypeStruct((1, unknowns, width), jnp.float32),
        ],
        in_specs=[vmem, vmem, vmem, vmem, smem, hbm, hbm],
        out_specs=[hbm, hbm],
        scratch_shapes=[
            pltpu.VMEM(high.shape, jnp.bfloat16),
            pltpu.VMEM(low.shape, jnp.bfloat16),
            [pltpu.VMEM((row_blocks, block_size, width), jnp.bfloat16)] * steps,
            pltpu.VMEM((steps, rows - 1, capacity, block_size, width), jnp.bfloat16),
            pltpu.VMEM((steps, rows, capacity, block_size, width), jnp.bfloat16),
            pltpu.VMEM((steps, unknowns, width), jnp.float32),
            pltpu.VMEM((steps, unknowns, width), jnp.float32),
            pltpu.VMEM((rows - 1,) + table.shape, jnp.int32),
            pltpu.SMEM((rows - 1,) + table.shape, jnp.int32),
            dma((steps, rows - 1)),
            dma((steps, rows - 1)),
            dma((steps, evens + 1)),
            dma((steps,)),
            dma((steps,)),
            dma((steps,)),
            dma((rows - 1,)),
            dma((rows - 1,)),
            dma((4,)),
            dma((steps,)),
        ],
        compiler_params=pltpu.CompilerParams(
            collective_id=0, has_side_effects=True, vmem_limit_bytes=48 * 1024 * 1024
        ),
    )(excitation, pending, inverse, table, needed[0], high, low)


def solution(mesh):
    in_specs = (
        P(None, "rows", None),
        P("lag", "rows", None),
        P("rows", None, None),
        P(("rows", "lag"), None, None),
        P(("rows", "lag")),
        P(("rows", "lag")),
        P(("rows", "lag")),
        P(("rows", "lag"), None, None),
        P("rows", "lag"),
    )
    out_specs = (P(None, "rows", None), P("lag", "rows", None))

    def body(*arrays):
        currents, carried = per_device(*arrays)
        return currents.reshape(arrays[0].shape), carried

    return jax.shard_map(body, mesh=mesh, in_specs=in_specs, out_specs=out_specs, check_vma=False)
```

```python
import functools

import jax
import jax.numpy as jnp
from jax import lax
from jax.experimental import pallas as pl
from jax.experimental.pallas import tpu as pltpu
from jax.sharding import PartitionSpec as P

MESH = pl.DeviceIdType.MESH


def split(value):
    high = value.astype(jnp.bfloat16)
    return high, (value - high.astype(jnp.float32)).astype(jnp.bfloat16)


def collapse_kernel(chunk, cell_ref, block_hbm, high_ref, low_ref, blocks, total, sems):
    columns, block_size = total.shape[1] // total.shape[2], total.shape[2]
    cells = total.shape[0] * columns
    slots = blocks.shape[0]

    def fetch(part):
        place = pl.ds(part * chunk, chunk)
        return pltpu.make_async_copy(block_hbm.at[place], blocks.at[place], sems.at[part])

    for part in range(slots // chunk):
        fetch(part).start()
    total[...] = jnp.zeros_like(total)
    live = cell_ref[slots]

    def add_slot(slot, carry):
        cell = cell_ref[slot]
        row = lax.div(cell, columns)
        start = pl.multiple_of(lax.rem(cell, columns) * block_size, block_size)
        total[row, pl.ds(start, block_size)] += blocks[slot].astype(jnp.float32)
        return carry

    for part in range(slots // chunk):
        fetch(part).wait()
        lax.fori_loop(part * chunk, jnp.clip(live, part * chunk, (part + 1) * chunk), add_slot, 0)

    for cell in range(cells):
        row, column = divmod(cell, columns)
        place = (pl.ds(row * block_size, block_size), pl.ds(column * block_size, block_size))
        high_ref[place], low_ref[place] = split(total[row, pl.ds(column * block_size, block_size)])


def collapse(interaction, slot_row, slot_owner, slot_pos, block_count, row_blocks, rows, capacity):
    slots, block_size, _ = interaction.shape
    columns = rows * capacity
    chunk = max(size for size in range(1, 17) if slots % size == 0)
    away = lax.rem(lax.axis_index("rows") + rows - slot_owner, rows)
    cell = slot_row * columns + away * capacity + slot_pos
    cell = jnp.concatenate([cell, block_count[0]])
    shape = (row_blocks * block_size, columns * block_size)
    vmem = pl.BlockSpec(memory_space=pltpu.VMEM)
    return pl.pallas_call(
        functools.partial(collapse_kernel, chunk),
        in_specs=[pl.BlockSpec(memory_space=pltpu.SMEM), pl.BlockSpec(memory_space=pltpu.HBM)],
        out_specs=[vmem, vmem],
        scratch_shapes=[
            pltpu.VMEM(interaction.shape, jnp.bfloat16),
            pltpu.VMEM((row_blocks, columns * block_size, block_size), jnp.float32),
            pltpu.SemaphoreType.DMA((slots // chunk,)),
        ],
        out_shape=[jax.ShapeDtypeStruct(shape, jnp.bfloat16)] * 2,
        compiler_params=pltpu.CompilerParams(vmem_limit_bytes=32 * 1024 * 1024),
    )(cell, interaction)


def window_kernel(
    rows, lags, steps, row_blocks, capacity,
    excitation, pending, inverse, table, high, low,
    currents, carried,
    solve_high, solve_low, own, sending, landed, handed, summed, asked, asked_scalar,
    row_send, row_recv, lag_send, lag_recv, hand_send, hand_recv, ask_send, ask_recv, local_sem, out_sem, gate,
):
    row = lax.axis_index("rows")
    lag = lax.axis_index("lag")
    block_size = inverse.shape[1]
    depth = capacity * block_size

    barrier = pltpu.get_barrier_semaphore()
    for away in range(1, rows):
        pl.semaphore_signal(barrier, inc=1, device_id=(lax.rem(row + away, rows), lag), device_id_type=MESH)
    for away in range(1, lags):
        pl.semaphore_signal(barrier, inc=1, device_id=(row, lax.rem(lag + away, lags)), device_id_type=MESH)

    own_table = pltpu.make_async_copy(table, asked_scalar.at[rows - 1], local_sem.at[0])
    own_table.start()

    def apply_inverse(block, value):
        return jnp.dot(
            inverse[block], value, precision=lax.Precision.HIGHEST, preferred_element_type=jnp.float32
        )

    def solved_part(step, before):
        parts = []
        for block in range(row_blocks):
            place = pl.ds(block * block_size, block_size)
            parts.append(apply_inverse(block, excitation[step, place].astype(jnp.float32) - before[place]))
        return jnp.concatenate(parts, axis=0)

    def keep_currents(step, value):
        own[step][...] = value.astype(jnp.bfloat16).reshape(own[step].shape)

    @pl.when(lag == 0)
    def _():
        keep_currents(0, solved_part(0, pending.at[0]))

    pl.semaphore_wait(barrier, rows + lags - 2)

    def ask_copy(away):
        target = lax.rem(row + away, rows)
        return pltpu.make_async_remote_copy(
            src_ref=table, dst_ref=asked.at[away - 1], send_sem=ask_send.at[away - 1],
            recv_sem=ask_recv.at[away - 1], device_id=(target, lag), device_id_type=MESH,
        )

    def row_copy(step, away):
        target = lax.rem(row + away, rows)
        return pltpu.make_async_remote_copy(
            src_ref=sending.at[step, away - 1], dst_ref=landed.at[step, away],
            send_sem=row_send.at[step, away - 1], recv_sem=row_recv.at[step, away - 1],
            device_id=(target, lag), device_id_type=MESH,
        )

    def lag_copy(step, target, which):
        return pltpu.make_async_remote_copy(
            src_ref=own[step], dst_ref=own[step],
            send_sem=lag_send.at[step, which], recv_sem=lag_recv.at[step],
            device_id=(row, target), device_id_type=MESH,
        )

    def hand_copy(step):
        source = pending.at[0] if step == 0 else summed.at[step - 1]
        return pltpu.make_async_remote_copy(
            src_ref=source, dst_ref=handed.at[step],
            send_sem=hand_send.at[step], recv_sem=hand_recv.at[step],
            device_id=(row, lax.rem(lag + lags - 1, lags)), device_id_type=MESH,
        )

    def out_copy(step):
        return pltpu.make_async_copy(own[step], currents.at[step], out_sem.at[step])

    def product_of(step, away, first, second):
        place = pl.ds(away * depth, depth)
        values = landed[step, away].reshape(depth, landed.shape[-1])
        return jnp.dot(first[:, place], values, preferred_element_type=jnp.float32) + jnp.dot(
            second[:, place], values, preferred_element_type=jnp.float32
        )

    def product(step, first, second):
        total = product_of(step, 0, first, second)
        for away in range(1, rows):
            row_copy(step, away).wait_recv()
            total += product_of(step, away, first, second)
        return total

    for away in range(1, rows):
        ask_copy(away).start()

    @pl.when(lag > 0)
    def _():
        hand_copy(0).start()

    @pl.when(lag == lags - 1)
    def _():
        handed[...] = jnp.zeros_like(handed)

    to_scalar = pltpu.make_async_copy(asked, asked_scalar.at[pl.ds(0, rows - 1)], local_sem.at[1])
    evens = list(range(2, lags, 2))
    forwards = (lag > 0) & (lax.rem(lag, 2) == 0) & (lag + 1 < lags)

    def send_evens(step):
        for place, target in enumerate(evens):
            lag_copy(step, target, place + 1).start()

    for step in range(steps):
        last = step == steps - 1

        @pl.when(lag > 0)
        def _():
            lag_copy(step, 0, 0).wait_recv()

        if step == 0:
            for away in range(1, rows):
                ask_copy(away).wait_recv()
            to_scalar.start()
            own_table.wait()
            to_scalar.wait()

        @pl.when(forwards)
        def _():
            lag_copy(step, lag + 1, 0).start()

        if last:
            @pl.when(lag == 0)
            def _():
                send_evens(step)
                lag_copy(step, 1, 0).start()

        for away in range(1, rows):
            for entry in range(capacity):
                sending[step, away - 1, entry] = own[step][asked_scalar[rows - away - 1, row, entry]]
        if not last:
            @pl.when(lag == 1)
            def _():
                pl.semaphore_wait(gate.at[step], 1)

        for away in range(1, rows):
            row_copy(step, away).start()

        if not last:
            @pl.when(lag == 0)
            def _():
                lag_copy(step, 1, 0).start()
                send_evens(step)

        out_copy(step).start()
        for entry in range(capacity):
            landed[step, 0, entry] = own[step][asked_scalar[rows - 1, row, entry]]

        if last:
            total = product(step, high, low)

            @pl.when(lag < lags - 1)
            def _():
                hand_copy(step).wait_recv()

            carried[0] = handed[step] + total
            continue

        @pl.when(lag == 0)
        def _():
            if step == 0:
                for block in range(row_blocks):
                    place = pl.ds(block * block_size, block_size)
                    value = high[place].astype(jnp.float32) + low[place].astype(jnp.float32)
                    solve_high[place], solve_low[place] = split(apply_inverse(block, value))
            hand_copy(step).wait_recv()
            base = solved_part(step + 1, handed.at[step])
            for away in range(1, rows):
                row_copy(step, away).wait_send()
            pl.semaphore_signal(gate.at[step], inc=1, device_id=(row, 1), device_id_type=MESH)
            keep_currents(step + 1, base - product(step, solve_high, solve_low))

        @pl.when(lag > 0)
        def _():
            total = product(step, high, low)

            @pl.when(lag < lags - 1)
            def _():
                hand_copy(step).wait_recv()

            summed[step] = handed[step] + total
            hand_copy(step + 1).start()

    for away in range(1, rows):
        ask_copy(away).wait_send()
    for step in range(steps):
        def wait_rows():
            for away in range(1, rows):
                row_copy(step, away).wait_send()

        if step == steps - 1:
            wait_rows()
        else:
            pl.when(lag > 0)(wait_rows)
        out_copy(step).wait()

        @pl.when(lag > 0)
        def _():
            hand_copy(step).wait_send()

        @pl.when(forwards)
        def _():
            lag_copy(step, lag + 1, 0).wait_send()

        @pl.when(lag == 0)
        def _():
            lag_copy(step, 1, 0).wait_send()
            for place, target in enumerate(evens):
                lag_copy(step, target, place + 1).wait_send()


def per_device(
    excitation, pending, inverse, interaction, slot_row, slot_owner, slot_pos, needed, block_count
):
    row_blocks, block_size, _ = inverse.shape
    steps, unknowns, width = excitation.shape
    rows, capacity = needed.shape[1:]
    lags = lax.axis_size("lag")
    high, low = collapse(
        interaction, slot_row, slot_owner, slot_pos, block_count, row_blocks, rows, capacity
    )
    table = jnp.pad(needed[0], ((0, -rows % 8), (0, -capacity % 128)))
    vmem = pl.BlockSpec(memory_space=pltpu.VMEM)
    dma = pltpu.SemaphoreType.DMA
    evens = len(range(2, lags, 2))
    return pl.pallas_call(
        functools.partial(window_kernel, rows, lags, steps, row_blocks, capacity),
        out_shape=[
            jax.ShapeDtypeStruct((steps, row_blocks, block_size, width), jnp.bfloat16),
            jax.ShapeDtypeStruct((1, unknowns, width), jnp.float32),
        ],
        in_specs=[vmem] * 6,
        out_specs=[vmem, vmem],
        scratch_shapes=[
            pltpu.VMEM(high.shape, jnp.bfloat16),
            pltpu.VMEM(low.shape, jnp.bfloat16),
            [pltpu.VMEM((row_blocks, block_size, width), jnp.bfloat16)] * steps,
            pltpu.VMEM((steps, rows - 1, capacity, block_size, width), jnp.bfloat16),
            pltpu.VMEM((steps, rows, capacity, block_size, width), jnp.bfloat16),
            pltpu.VMEM((steps, unknowns, width), jnp.float32),
            pltpu.VMEM((steps, unknowns, width), jnp.float32),
            pltpu.VMEM((rows - 1,) + table.shape, jnp.int32),
            pltpu.SMEM((rows,) + table.shape, jnp.int32),
            dma((steps, rows - 1)),
            dma((steps, rows - 1)),
            dma((steps, evens + 1)),
            dma((steps,)),
            dma((steps,)),
            dma((steps,)),
            dma((rows - 1,)),
            dma((rows - 1,)),
            dma((2,)),
            dma((steps,)),
            pltpu.SemaphoreType.REGULAR((steps,)),
        ],
        compiler_params=pltpu.CompilerParams(
            collective_id=0, has_side_effects=True, vmem_limit_bytes=48 * 1024 * 1024
        ),
    )(excitation, pending, inverse, table, high, low)


def solution(mesh):
    in_specs = (
        P(None, "rows", None),
        P("lag", "rows", None),
        P("rows", None, None),
        P(("rows", "lag"), None, None),
        P(("rows", "lag")),
        P(("rows", "lag")),
        P(("rows", "lag")),
        P(("rows", "lag"), None, None),
        P("rows", "lag"),
    )
    out_specs = (P(None, "rows", None), P("lag", "rows", None))

    def body(*arrays):
        currents, carried = per_device(*arrays)
        return currents.reshape(arrays[0].shape), carried

    return jax.shard_map(body, mesh=mesh, in_specs=in_specs, out_specs=out_specs, check_vma=False)
```

```python
import functools

import jax
import jax.numpy as jnp
from jax import lax
from jax.experimental import pallas as pl
from jax.experimental.pallas import tpu as pltpu
from jax.sharding import PartitionSpec as P

MESH = pl.DeviceIdType.MESH


def split(value):
    high = value.astype(jnp.bfloat16)
    return high, (value - high.astype(jnp.float32)).astype(jnp.bfloat16)


def collapse_kernel(chunk, cell_ref, block_hbm, high_ref, low_ref, blocks, total, sems):
    columns, block_size = total.shape[1] // total.shape[2], total.shape[2]
    cells = total.shape[0] * columns
    slots = blocks.shape[0]

    def fetch(part):
        place = pl.ds(part * chunk, chunk)
        return pltpu.make_async_copy(block_hbm.at[place], blocks.at[place], sems.at[part])

    for part in range(slots // chunk):
        fetch(part).start()
    total[...] = jnp.zeros_like(total)
    live = cell_ref[slots]

    def add_slot(slot, carry):
        cell = cell_ref[slot]
        row = lax.div(cell, columns)
        start = pl.multiple_of(lax.rem(cell, columns) * block_size, block_size)
        total[row, pl.ds(start, block_size)] += blocks[slot].astype(jnp.float32)
        return carry

    for part in range(slots // chunk):
        fetch(part).wait()
        lax.fori_loop(part * chunk, jnp.clip(live, part * chunk, (part + 1) * chunk), add_slot, 0)

    for cell in range(cells):
        row, column = divmod(cell, columns)
        place = (pl.ds(row * block_size, block_size), pl.ds(column * block_size, block_size))
        high_ref[place], low_ref[place] = split(total[row, pl.ds(column * block_size, block_size)])


def collapse(interaction, slot_row, slot_owner, slot_pos, block_count, row_blocks, rows, capacity):
    slots, block_size, _ = interaction.shape
    columns = rows * capacity
    chunk = max(size for size in range(1, 17) if slots % size == 0)
    away = lax.rem(lax.axis_index("rows") + rows - slot_owner, rows)
    cell = slot_row * columns + away * capacity + slot_pos
    cell = jnp.concatenate([cell, block_count[0]])
    shape = (row_blocks * block_size, columns * block_size)
    vmem = pl.BlockSpec(memory_space=pltpu.VMEM)
    return pl.pallas_call(
        functools.partial(collapse_kernel, chunk),
        in_specs=[pl.BlockSpec(memory_space=pltpu.SMEM), pl.BlockSpec(memory_space=pltpu.HBM)],
        out_specs=[vmem, vmem],
        scratch_shapes=[
            pltpu.VMEM(interaction.shape, jnp.bfloat16),
            pltpu.VMEM((row_blocks, columns * block_size, block_size), jnp.float32),
            pltpu.SemaphoreType.DMA((slots // chunk,)),
        ],
        out_shape=[jax.ShapeDtypeStruct(shape, jnp.bfloat16)] * 2,
        compiler_params=pltpu.CompilerParams(vmem_limit_bytes=60 * 1024 * 1024),
    )(cell, interaction)


def window_kernel(
    rows, lags, steps, row_blocks, capacity,
    excitation, pending, inverse, table, high, low,
    currents, carried,
    solve_high, solve_low, own, sending, landed, handed, summed, asked, asked_scalar,
    row_send, row_recv, lag_send, lag_recv, hand_send, hand_recv, ask_send, ask_recv, local_sem, out_sem, gate,
):
    row = lax.axis_index("rows")
    lag = lax.axis_index("lag")
    block_size = inverse.shape[1]
    depth = capacity * block_size
    pieces = [len(own[step]) for step in range(steps)]

    def rows_of(step, piece):
        size = block_size // pieces[step]
        return pl.ds(piece * size, size)

    barrier = pltpu.get_barrier_semaphore()
    for away in range(1, rows):
        pl.semaphore_signal(barrier, inc=1, device_id=(lax.rem(row + away, rows), lag), device_id_type=MESH)
    for away in range(1, lags):
        pl.semaphore_signal(barrier, inc=1, device_id=(row, lax.rem(lag + away, lags)), device_id_type=MESH)

    own_table = pltpu.make_async_copy(table, asked_scalar.at[rows - 1], local_sem.at[0])
    own_table.start()

    def apply_inverse(block, value):
        return jnp.dot(
            inverse[block], value, precision=lax.Precision.HIGHEST, preferred_element_type=jnp.float32
        )

    def solved_part(step, before):
        parts = []
        for block in range(row_blocks):
            place = pl.ds(block * block_size, block_size)
            parts.append(apply_inverse(block, excitation[step, place].astype(jnp.float32) - before[place]))
        return jnp.concatenate(parts, axis=0)

    def keep_currents(step, value):
        value = value.astype(jnp.bfloat16).reshape(row_blocks, block_size, value.shape[-1])
        size = block_size // pieces[step]
        for piece in range(pieces[step]):
            own[step][piece][...] = value[:, piece * size : (piece + 1) * size]

    @pl.when(lag == 0)
    def _():
        keep_currents(0, solved_part(0, pending.at[0]))

    pl.semaphore_wait(barrier, rows + lags - 2)

    def ask_copy(away):
        target = lax.rem(row + away, rows)
        return pltpu.make_async_remote_copy(
            src_ref=table, dst_ref=asked.at[away - 1], send_sem=ask_send.at[away - 1],
            recv_sem=ask_recv.at[away - 1], device_id=(target, lag), device_id_type=MESH,
        )

    def row_copy(step, piece, away):
        target = lax.rem(row + away, rows)
        return pltpu.make_async_remote_copy(
            src_ref=sending.at[step, away - 1, :, rows_of(step, piece)],
            dst_ref=landed.at[step, away, :, rows_of(step, piece)],
            send_sem=row_send.at[step, piece, away - 1], recv_sem=row_recv.at[step, piece, away - 1],
            device_id=(target, lag), device_id_type=MESH,
        )

    def lag_copy(step, piece, target, which):
        return pltpu.make_async_remote_copy(
            src_ref=own[step][piece], dst_ref=own[step][piece],
            send_sem=lag_send.at[step, piece, which], recv_sem=lag_recv.at[step, piece],
            device_id=(row, target), device_id_type=MESH,
        )

    def hand_copy(step):
        source = pending.at[0] if step == 0 else summed.at[step - 1]
        return pltpu.make_async_remote_copy(
            src_ref=source, dst_ref=handed.at[step],
            send_sem=hand_send.at[step], recv_sem=hand_recv.at[step],
            device_id=(row, lax.rem(lag + lags - 1, lags)), device_id_type=MESH,
        )

    def out_copy(step, piece):
        return pltpu.make_async_copy(
            own[step][piece], currents.at[step, :, rows_of(step, piece)], out_sem.at[step, piece]
        )

    def product_of(step, away, first, second):
        place = pl.ds(away * depth, depth)
        values = landed[step, away].reshape(depth, landed.shape[-1])
        return jnp.dot(first[:, place], values, preferred_element_type=jnp.float32) + jnp.dot(
            second[:, place], values, preferred_element_type=jnp.float32
        )

    def product(step, first, second):
        total = product_of(step, 0, first, second)
        for away in range(1, rows):
            for piece in range(pieces[step]):
                row_copy(step, piece, away).wait_recv()
            total += product_of(step, away, first, second)
        return total

    for away in range(1, rows):
        ask_copy(away).start()

    @pl.when(lag > 0)
    def _():
        hand_copy(0).start()

    @pl.when(lag == lags - 1)
    def _():
        handed[...] = jnp.zeros_like(handed)

    to_scalar = pltpu.make_async_copy(asked, asked_scalar.at[pl.ds(0, rows - 1)], local_sem.at[1])
    evens = list(range(2, lags, 2))
    forwards = (lag > 0) & (lax.rem(lag, 2) == 0) & (lag + 1 < lags)

    def send_evens(step, piece):
        for place, target in enumerate(evens):
            lag_copy(step, piece, target, place + 1).start()

    for step in range(steps):
        last = step == steps - 1

        if last:
            @pl.when(lag == 0)
            def _():
                for piece in range(pieces[step]):
                    send_evens(step, piece)
                    lag_copy(step, piece, 1, 0).start()

        for piece in range(pieces[step]):
            @pl.when(lag > 0)
            def _():
                lag_copy(step, piece, 0, 0).wait_recv()

            if step == 0:
                for away in range(1, rows):
                    ask_copy(away).wait_recv()
                to_scalar.start()
                own_table.wait()
                to_scalar.wait()

            @pl.when(forwards)
            def _():
                lag_copy(step, piece, lag + 1, 0).start()

            place = rows_of(step, piece)
            for away in range(1, rows):
                for entry in range(capacity):
                    block = asked_scalar[rows - away - 1, row, entry]
                    sending[step, away - 1, entry, place] = own[step][piece][block]
            if not last:
                @pl.when(lag == 1)
                def _():
                    pl.semaphore_wait(gate.at[step], 1)

            for away in range(1, rows):
                row_copy(step, piece, away).start()

            if not last:
                @pl.when(lag == 0)
                def _():
                    lag_copy(step, piece, 1, 0).start()
                    send_evens(step, piece)

            out_copy(step, piece).start()
            for entry in range(capacity):
                landed[step, 0, entry, place] = own[step][piece][asked_scalar[rows - 1, row, entry]]

        if last:
            total = product(step, high, low)

            @pl.when(lag < lags - 1)
            def _():
                hand_copy(step).wait_recv()

            carried[0] = handed[step] + total
            continue

        @pl.when(lag == 0)
        def _():
            if step == 0:
                for block in range(row_blocks):
                    place = pl.ds(block * block_size, block_size)
                    value = high[place].astype(jnp.float32) + low[place].astype(jnp.float32)
                    solve_high[place], solve_low[place] = split(apply_inverse(block, value))
            for away in range(1, rows):
                row_copy(step, 0, away).wait_send()
            pl.semaphore_signal(gate.at[step], inc=1, device_id=(row, 1), device_id_type=MESH)
            hand_copy(step).wait_recv()
            base = solved_part(step + 1, handed.at[step])
            keep_currents(step + 1, base - product(step, solve_high, solve_low))

        @pl.when(lag > 0)
        def _():
            total = product(step, high, low)

            @pl.when(lag < lags - 1)
            def _():
                hand_copy(step).wait_recv()

            summed[step] = handed[step] + total
            hand_copy(step + 1).start()

    for away in range(1, rows):
        ask_copy(away).wait_send()
    for step in range(steps):
        @pl.when(lag > 0)
        def _():
            hand_copy(step).wait_send()

        for piece in range(pieces[step]):
            def wait_rows():
                for away in range(1, rows):
                    row_copy(step, piece, away).wait_send()

            if step == steps - 1:
                wait_rows()
            else:
                pl.when(lag > 0)(wait_rows)
            out_copy(step, piece).wait()

            @pl.when(forwards)
            def _():
                lag_copy(step, piece, lag + 1, 0).wait_send()

            @pl.when(lag == 0)
            def _():
                lag_copy(step, piece, 1, 0).wait_send()
                for place, target in enumerate(evens):
                    lag_copy(step, piece, target, place + 1).wait_send()


def per_device(
    excitation, pending, inverse, interaction, slot_row, slot_owner, slot_pos, needed, block_count
):
    row_blocks, block_size, _ = inverse.shape
    steps, unknowns, width = excitation.shape
    rows, capacity = needed.shape[1:]
    lags = lax.axis_size("lag")
    high, low = collapse(
        interaction, slot_row, slot_owner, slot_pos, block_count, row_blocks, rows, capacity
    )
    table = jnp.pad(needed[0], ((0, -rows % 8), (0, -capacity % 128)))
    vmem = pl.BlockSpec(memory_space=pltpu.VMEM)
    dma = pltpu.SemaphoreType.DMA
    evens = len(range(2, lags, 2))
    tail = 2 if block_size % 32 == 0 else 1
    return pl.pallas_call(
        functools.partial(window_kernel, rows, lags, steps, row_blocks, capacity),
        out_shape=[
            jax.ShapeDtypeStruct((steps, row_blocks, block_size, width), jnp.bfloat16),
            jax.ShapeDtypeStruct((1, unknowns, width), jnp.float32),
        ],
        in_specs=[vmem] * 6,
        out_specs=[vmem, vmem],
        scratch_shapes=[
            pltpu.VMEM(high.shape, jnp.bfloat16),
            pltpu.VMEM(low.shape, jnp.bfloat16),
            [
                [pltpu.VMEM((row_blocks, block_size // cut, width), jnp.bfloat16)] * cut
                for cut in [1] * (steps - 1) + [tail]
            ],
            pltpu.VMEM((steps, rows - 1, capacity, block_size, width), jnp.bfloat16),
            pltpu.VMEM((steps, rows, capacity, block_size, width), jnp.bfloat16),
            pltpu.VMEM((steps, unknowns, width), jnp.float32),
            pltpu.VMEM((steps, unknowns, width), jnp.float32),
            pltpu.VMEM((rows - 1,) + table.shape, jnp.int32),
            pltpu.SMEM((rows,) + table.shape, jnp.int32),
            dma((steps, tail, rows - 1)),
            dma((steps, tail, rows - 1)),
            dma((steps, tail, evens + 1)),
            dma((steps, tail)),
            dma((steps,)),
            dma((steps,)),
            dma((rows - 1,)),
            dma((rows - 1,)),
            dma((2,)),
            dma((steps, tail)),
            pltpu.SemaphoreType.REGULAR((steps,)),
        ],
        compiler_params=pltpu.CompilerParams(
            collective_id=0, has_side_effects=True, vmem_limit_bytes=48 * 1024 * 1024
        ),
    )(excitation, pending, inverse, table, high, low)


def solution(mesh):
    in_specs = (
        P(None, "rows", None),
        P("lag", "rows", None),
        P("rows", None, None),
        P(("rows", "lag"), None, None),
        P(("rows", "lag")),
        P(("rows", "lag")),
        P(("rows", "lag")),
        P(("rows", "lag"), None, None),
        P("rows", "lag"),
    )
    out_specs = (P(None, "rows", None), P("lag", "rows", None))

    def body(*arrays):
        currents, carried = per_device(*arrays)
        return currents.reshape(arrays[0].shape), carried

    return jax.shard_map(body, mesh=mesh, in_specs=in_specs, out_specs=out_specs, check_vma=False)
```

```python
import functools

import jax
import jax.numpy as jnp
from jax import lax
from jax.experimental import pallas as pl
from jax.experimental.pallas import tpu as pltpu
from jax.sharding import PartitionSpec as P

MESH = pl.DeviceIdType.MESH


def split(value):
    high = value.astype(jnp.bfloat16)
    return high, (value - high.astype(jnp.float32)).astype(jnp.bfloat16)


def collapse_kernel(chunk, cell_ref, block_hbm, high_ref, low_ref, blocks, total, sems):
    columns, block_size = total.shape[1] // total.shape[2], total.shape[2]
    cells = total.shape[0] * columns
    slots = blocks.shape[0]

    def fetch(part):
        place = pl.ds(part * chunk, chunk)
        return pltpu.make_async_copy(block_hbm.at[place], blocks.at[place], sems.at[part])

    for part in range(slots // chunk):
        fetch(part).start()
    total[...] = jnp.zeros_like(total)
    live = cell_ref[slots]

    def add_slot(slot, carry):
        cell = cell_ref[slot]
        row = lax.div(cell, columns)
        start = pl.multiple_of(lax.rem(cell, columns) * block_size, block_size)
        total[row, pl.ds(start, block_size)] += blocks[slot].astype(jnp.float32)
        return carry

    for part in range(slots // chunk):
        fetch(part).wait()
        lax.fori_loop(part * chunk, jnp.clip(live, part * chunk, (part + 1) * chunk), add_slot, 0)

    for cell in range(cells):
        row, column = divmod(cell, columns)
        place = (pl.ds(row * block_size, block_size), pl.ds(column * block_size, block_size))
        high_ref[place], low_ref[place] = split(total[row, pl.ds(column * block_size, block_size)])


def collapse(interaction, slot_row, slot_owner, slot_pos, block_count, row_blocks, rows, capacity):
    slots, block_size, _ = interaction.shape
    columns = rows * capacity
    chunk = max(size for size in range(1, 17) if slots % size == 0)
    away = lax.rem(lax.axis_index("rows") + rows - slot_owner, rows)
    cell = slot_row * columns + away * capacity + slot_pos
    cell = jnp.concatenate([cell, block_count[0]])
    shape = (row_blocks * block_size, columns * block_size)
    vmem = pl.BlockSpec(memory_space=pltpu.VMEM)
    return pl.pallas_call(
        functools.partial(collapse_kernel, chunk),
        in_specs=[pl.BlockSpec(memory_space=pltpu.SMEM), pl.BlockSpec(memory_space=pltpu.HBM)],
        out_specs=[vmem, vmem],
        scratch_shapes=[
            pltpu.VMEM(interaction.shape, jnp.bfloat16),
            pltpu.VMEM((row_blocks, columns * block_size, block_size), jnp.float32),
            pltpu.SemaphoreType.DMA((slots // chunk,)),
        ],
        out_shape=[jax.ShapeDtypeStruct(shape, jnp.bfloat16)] * 2,
        compiler_params=pltpu.CompilerParams(vmem_limit_bytes=32 * 1024 * 1024),
    )(cell, interaction)


def window_kernel(
    rows, lags, steps, row_blocks, capacity,
    excitation, pending, inverse, table, high, low,
    currents, carried,
    solve_high, solve_low, own, whole, sending, landed, handed, summed, asked, asked_scalar,
    row_send, row_recv, lag_send, lag_recv, hand_send, hand_recv, ask_send, ask_recv, local_sem, out_sem, gate,
    spread_send, along_send, gather_send, gather_recv, odd_send, odd_recv,
):
    row = lax.axis_index("rows")
    lag = lax.axis_index("lag")
    block_size = inverse.shape[1]
    depth = capacity * block_size
    final = steps - 1
    own = list(own) + [whole[0]]
    pairs = lags // 2
    pair = lax.div(lag, 2)
    even = lax.rem(lag, 2) == 0
    cuts = whole[0].shape[1]
    each = row_blocks * cuts // pairs

    def picked(ref, index):
        return ref[index].reshape(block_size, ref.shape[-1])

    def piece_of(ref, index):
        if cuts > 1:
            return ref.at[lax.div(index, cuts), lax.rem(index, cuts)]
        return ref.at[pl.ds(index * each, each)]

    barrier = pltpu.get_barrier_semaphore()
    for away in range(1, rows):
        pl.semaphore_signal(barrier, inc=1, device_id=(lax.rem(row + away, rows), lag), device_id_type=MESH)
    for away in range(1, lags):
        pl.semaphore_signal(barrier, inc=1, device_id=(row, lax.rem(lag + away, lags)), device_id_type=MESH)

    own_table = pltpu.make_async_copy(table, asked_scalar.at[rows - 1], local_sem.at[0])
    own_table.start()

    def apply_inverse(block, value):
        return jnp.dot(
            inverse[block], value, precision=lax.Precision.HIGHEST, preferred_element_type=jnp.float32
        )

    def solved_part(step, before):
        parts = []
        for block in range(row_blocks):
            place = pl.ds(block * block_size, block_size)
            parts.append(apply_inverse(block, excitation[step, place].astype(jnp.float32) - before[place]))
        return jnp.concatenate(parts, axis=0)

    def keep_currents(step, value):
        own[step][...] = value.astype(jnp.bfloat16).reshape(own[step].shape)

    @pl.when(lag == 0)
    def _():
        keep_currents(0, solved_part(0, pending.at[0]))

    pl.semaphore_wait(barrier, rows + lags - 2)

    def ask_copy(away):
        target = lax.rem(row + away, rows)
        return pltpu.make_async_remote_copy(
            src_ref=table, dst_ref=asked.at[away - 1], send_sem=ask_send.at[away - 1],
            recv_sem=ask_recv.at[away - 1], device_id=(target, lag), device_id_type=MESH,
        )

    def row_copy(step, away):
        target = lax.rem(row + away, rows)
        return pltpu.make_async_remote_copy(
            src_ref=sending.at[step, away - 1], dst_ref=landed.at[step, away],
            send_sem=row_send.at[step, away - 1], recv_sem=row_recv.at[step, away - 1],
            device_id=(target, lag), device_id_type=MESH,
        )

    def lag_copy(step, target, which):
        return pltpu.make_async_remote_copy(
            src_ref=own[step], dst_ref=own[step],
            send_sem=lag_send.at[step, which], recv_sem=lag_recv.at[step],
            device_id=(row, target), device_id_type=MESH,
        )

    def hand_copy(step):
        source = pending.at[0] if step == 0 else summed.at[step - 1]
        return pltpu.make_async_remote_copy(
            src_ref=source, dst_ref=handed.at[step],
            send_sem=hand_send.at[step], recv_sem=hand_recv.at[step],
            device_id=(row, lax.rem(lag + lags - 1, lags)), device_id_type=MESH,
        )

    def out_copy(step):
        return pltpu.make_async_copy(own[step], currents.at[step], out_sem.at[step])

    def product_of(step, away, first, second):
        place = pl.ds(away * depth, depth)
        values = landed[step, away].reshape(depth, landed.shape[-1])
        return jnp.dot(first[:, place], values, preferred_element_type=jnp.float32) + jnp.dot(
            second[:, place], values, preferred_element_type=jnp.float32
        )

    def product(step, first, second):
        total = product_of(step, 0, first, second)
        for away in range(1, rows):
            row_copy(step, away).wait_recv()
            total += product_of(step, away, first, second)
        return total

    for away in range(1, rows):
        ask_copy(away).start()

    @pl.when(lag > 0)
    def _():
        hand_copy(0).start()

    @pl.when(lag == lags - 1)
    def _():
        handed[...] = jnp.zeros_like(handed)

    to_scalar = pltpu.make_async_copy(asked, asked_scalar.at[pl.ds(0, rows - 1)], local_sem.at[1])
    evens = list(range(2, lags, 2))
    forwards = (lag > 0) & (lax.rem(lag, 2) == 0) & (lag + 1 < lags)

    def send_evens(step):
        for place, target in enumerate(evens):
            lag_copy(step, target, place + 1).start()

    for step in range(final):
        @pl.when(lag > 0)
        def _():
            lag_copy(step, 0, 0).wait_recv()

        if step == 0:
            for away in range(1, rows):
                ask_copy(away).wait_recv()
            to_scalar.start()
            own_table.wait()
            to_scalar.wait()

        @pl.when(forwards)
        def _():
            lag_copy(step, lag + 1, 0).start()

        for away in range(1, rows):
            for entry in range(capacity):
                sending[step, away - 1, entry] = picked(own[step], asked_scalar[rows - away - 1, row, entry])

        @pl.when(lag == 1)
        def _():
            pl.semaphore_wait(gate.at[step], 1)

        for away in range(1, rows):
            row_copy(step, away).start()

        @pl.when(lag == 0)
        def _():
            lag_copy(step, 1, 0).start()
            send_evens(step)

        out_copy(step).start()
        for entry in range(capacity):
            landed[step, 0, entry] = picked(own[step], asked_scalar[rows - 1, row, entry])

        @pl.when(lag == 0)
        def _():
            if step == 0:
                for block in range(row_blocks):
                    place = pl.ds(block * block_size, block_size)
                    value = high[place].astype(jnp.float32) + low[place].astype(jnp.float32)
                    solve_high[place], solve_low[place] = split(apply_inverse(block, value))
            for away in range(1, rows):
                row_copy(step, away).wait_send()
            pl.semaphore_signal(gate.at[step], inc=1, device_id=(row, 1), device_id_type=MESH)
            hand_copy(step).wait_recv()
            base = solved_part(step + 1, handed.at[step])
            keep_currents(step + 1, base - product(step, solve_high, solve_low))

        @pl.when(lag > 0)
        def _():
            total = product(step, high, low)

            @pl.when(lag < lags - 1)
            def _():
                hand_copy(step).wait_recv()

            summed[step] = handed[step] + total
            hand_copy(step + 1).start()

    def spread_copy(target):
        return pltpu.make_async_remote_copy(
            src_ref=piece_of(whole[0], target), dst_ref=piece_of(whole[0], target),
            send_sem=spread_send.at[target], recv_sem=gather_recv.at[0, target],
            device_id=(row, 2 * target), device_id_type=MESH,
        )

    def along_copy(away):
        return pltpu.make_async_remote_copy(
            src_ref=piece_of(whole[0], pair), dst_ref=piece_of(whole[away], pair),
            send_sem=along_send.at[away - 1], recv_sem=gather_recv.at[away, pair],
            device_id=(lax.rem(row + away, rows), lag), device_id_type=MESH,
        )

    def gather_copy(away, turn):
        return pltpu.make_async_remote_copy(
            src_ref=piece_of(whole[away], pair), dst_ref=piece_of(whole[away], pair),
            send_sem=gather_send.at[away, turn - 1], recv_sem=gather_recv.at[away, pair],
            device_id=(row, 2 * lax.rem(pair + turn, pairs)), device_id_type=MESH,
        )

    def arrival(away, source):
        return pltpu.make_async_remote_copy(
            src_ref=piece_of(whole[away], source), dst_ref=piece_of(whole[away], source),
            send_sem=gather_send.at[away, 0], recv_sem=gather_recv.at[away, source],
            device_id=(row, lax.rem(lag + 2, lags)), device_id_type=MESH,
        )

    def odd_copy(away):
        return pltpu.make_async_remote_copy(
            src_ref=whole[away], dst_ref=whole[away],
            send_sem=odd_send.at[away], recv_sem=odd_recv.at[away],
            device_id=(row, lax.rem(lag + 1, lags)), device_id_type=MESH,
        )

    @pl.when(lag == 0)
    def _():
        for target in range(1, pairs):
            spread_copy(target).start()
        odd_copy(0).start()

    @pl.when(even)
    def _():
        @pl.when(lag > 0)
        def _():
            arrival(0, pair).wait_recv()

        for away in range(1, rows):
            along_copy(away).start()
        for turn in range(1, pairs):
            @pl.when(lax.rem(pair + turn, pairs) > 0)
            def _():
                gather_copy(0, turn).start()
        for away in range(1, rows):
            arrival(away, pair).wait_recv()
            for turn in range(1, pairs):
                gather_copy(away, turn).start()

    total = None
    for away in range(rows):
        @pl.when(even if away > 0 else even & (lag > 0))
        def _():
            for turn in range(1, pairs):
                arrival(away, lax.rem(pair + turn, pairs)).wait_recv()
            odd_copy(away).start()

        @pl.when(jnp.logical_not(even))
        def _():
            odd_copy(away).wait_recv()

        if away == 0:
            out_copy(final).start()
        source = lax.rem(row + rows - away, rows)
        for entry in range(capacity):
            landed[final, away, entry] = picked(whole[away], asked_scalar[rows - 1, source, entry])
        part = product_of(final, away, high, low)
        total = part if total is None else total + part

    @pl.when(lag < lags - 1)
    def _():
        hand_copy(final).wait_recv()

    carried[0] = handed[final] + total

    for away in range(1, rows):
        ask_copy(away).wait_send()
    for step in range(steps):
        out_copy(step).wait()

        @pl.when(lag > 0)
        def _():
            hand_copy(step).wait_send()
            if step < final:
                for away in range(1, rows):
                    row_copy(step, away).wait_send()

        if step < final:
            @pl.when(forwards)
            def _():
                lag_copy(step, lag + 1, 0).wait_send()

            @pl.when(lag == 0)
            def _():
                lag_copy(step, 1, 0).wait_send()
                for place, target in enumerate(evens):
                    lag_copy(step, target, place + 1).wait_send()

    @pl.when(lag == 0)
    def _():
        for target in range(1, pairs):
            spread_copy(target).wait_send()

    @pl.when(even)
    def _():
        for away in range(1, rows):
            along_copy(away).wait_send()
        for away in range(rows):
            odd_copy(away).wait_send()
            for turn in range(1, pairs):
                @pl.when((lax.rem(pair + turn, pairs) > 0) | (away > 0))
                def _():
                    gather_copy(away, turn).wait_send()


def per_device(
    excitation, pending, inverse, interaction, slot_row, slot_owner, slot_pos, needed, block_count
):
    row_blocks, block_size, _ = inverse.shape
    steps, unknowns, width = excitation.shape
    rows, capacity = needed.shape[1:]
    lags = lax.axis_size("lag")
    high, low = collapse(
        interaction, slot_row, slot_owner, slot_pos, block_count, row_blocks, rows, capacity
    )
    table = jnp.pad(needed[0], ((0, -rows % 8), (0, -capacity % 128)))
    vmem = pl.BlockSpec(memory_space=pltpu.VMEM)
    dma = pltpu.SemaphoreType.DMA
    evens = len(range(2, lags, 2))
    cuts = max(1, lags // 2 // row_blocks)
    shape = (row_blocks, cuts, block_size // cuts, width)
    return pl.pallas_call(
        functools.partial(window_kernel, rows, lags, steps, row_blocks, capacity),
        out_shape=[
            jax.ShapeDtypeStruct((steps,) + shape, jnp.bfloat16),
            jax.ShapeDtypeStruct((1, unknowns, width), jnp.float32),
        ],
        in_specs=[vmem] * 6,
        out_specs=[vmem, vmem],
        scratch_shapes=[
            pltpu.VMEM(high.shape, jnp.bfloat16),
            pltpu.VMEM(low.shape, jnp.bfloat16),
            [pltpu.VMEM(shape, jnp.bfloat16)] * (steps - 1),
            [pltpu.VMEM(shape, jnp.bfloat16)] * rows,
            pltpu.VMEM((steps, rows - 1, capacity, block_size, width), jnp.bfloat16),
            pltpu.VMEM((steps, rows, capacity, block_size, width), jnp.bfloat16),
            pltpu.VMEM((steps, unknowns, width), jnp.float32),
            pltpu.VMEM((steps, unknowns, width), jnp.float32),
            pltpu.VMEM((rows - 1,) + table.shape, jnp.int32),
            pltpu.SMEM((rows,) + table.shape, jnp.int32),
            dma((steps, rows - 1)),
            dma((steps, rows - 1)),
            dma((steps, evens + 1)),
            dma((steps,)),
            dma((steps,)),
            dma((steps,)),
            dma((rows - 1,)),
            dma((rows - 1,)),
            dma((2,)),
            dma((steps,)),
            pltpu.SemaphoreType.REGULAR((steps,)),
            dma((lags // 2,)),
            dma((rows,)),
            dma((rows, lags // 2)),
            dma((rows, lags // 2)),
            dma((rows,)),
            dma((rows,)),
        ],
        compiler_params=pltpu.CompilerParams(
            collective_id=0, has_side_effects=True, vmem_limit_bytes=48 * 1024 * 1024
        ),
    )(excitation, pending, inverse, table, high, low)


def solution(mesh):
    in_specs = (
        P(None, "rows", None),
        P("lag", "rows", None),
        P("rows", None, None),
        P(("rows", "lag"), None, None),
        P(("rows", "lag")),
        P(("rows", "lag")),
        P(("rows", "lag")),
        P(("rows", "lag"), None, None),
        P("rows", "lag"),
    )
    out_specs = (P(None, "rows", None), P("lag", "rows", None))

    def body(*arrays):
        currents, carried = per_device(*arrays)
        return currents.reshape(arrays[0].shape), carried

    return jax.shard_map(body, mesh=mesh, in_specs=in_specs, out_specs=out_specs, check_vma=False)
```

```python
import functools

import jax
import jax.numpy as jnp
from jax import lax
from jax.experimental import pallas as pl
from jax.experimental.pallas import tpu as pltpu
from jax.sharding import PartitionSpec as P

MESH = pl.DeviceIdType.MESH


def split(value):
    high = value.astype(jnp.bfloat16)
    return high, (value - high.astype(jnp.float32)).astype(jnp.bfloat16)


def collapse_kernel(chunk, cell_ref, block_hbm, high_ref, low_ref, blocks, total, sems):
    columns, block_size = total.shape[1] // total.shape[2], total.shape[2]
    cells = total.shape[0] * columns
    slots = blocks.shape[0]

    def fetch(part):
        place = pl.ds(part * chunk, chunk)
        return pltpu.make_async_copy(block_hbm.at[place], blocks.at[place], sems.at[part])

    for part in range(slots // chunk):
        fetch(part).start()
    total[...] = jnp.zeros_like(total)
    live = cell_ref[slots]

    def add_slot(slot, carry):
        cell = cell_ref[slot]
        row = lax.div(cell, columns)
        start = pl.multiple_of(lax.rem(cell, columns) * block_size, block_size)
        total[row, pl.ds(start, block_size)] += blocks[slot].astype(jnp.float32)
        return carry

    for part in range(slots // chunk):
        fetch(part).wait()
        lax.fori_loop(part * chunk, jnp.clip(live, part * chunk, (part + 1) * chunk), add_slot, 0)

    for cell in range(cells):
        row, column = divmod(cell, columns)
        place = (pl.ds(row * block_size, block_size), pl.ds(column * block_size, block_size))
        high_ref[place], low_ref[place] = split(total[row, pl.ds(column * block_size, block_size)])


def collapse(interaction, slot_row, slot_owner, slot_pos, block_count, row_blocks, rows, capacity):
    slots, block_size, _ = interaction.shape
    columns = rows * capacity
    chunk = max(size for size in range(1, 17) if slots % size == 0)
    away = lax.rem(lax.axis_index("rows") + rows - slot_owner, rows)
    cell = slot_row * columns + away * capacity + slot_pos
    cell = jnp.concatenate([cell, block_count[0]])
    shape = (row_blocks * block_size, columns * block_size)
    vmem = pl.BlockSpec(memory_space=pltpu.VMEM)
    return pl.pallas_call(
        functools.partial(collapse_kernel, chunk),
        in_specs=[pl.BlockSpec(memory_space=pltpu.SMEM), pl.BlockSpec(memory_space=pltpu.HBM)],
        out_specs=[vmem, vmem],
        scratch_shapes=[
            pltpu.VMEM(interaction.shape, jnp.bfloat16),
            pltpu.VMEM((row_blocks, columns * block_size, block_size), jnp.float32),
            pltpu.SemaphoreType.DMA((slots // chunk,)),
        ],
        out_shape=[jax.ShapeDtypeStruct(shape, jnp.bfloat16)] * 2,
        compiler_params=pltpu.CompilerParams(vmem_limit_bytes=50 * 1024 * 1024),
    )(cell, interaction)


def window_kernel(
    rows, lags, steps, row_blocks, capacity,
    excitation, pending, inverse, table, high, low,
    currents, carried,
    solve_high, solve_low, own, sending, landed, handed, summed, asked, asked_scalar,
    row_send, row_recv, lag_send, lag_recv, hand_send, hand_recv, ask_send, ask_recv, local_sem, out_sem,
):
    row = lax.axis_index("rows")
    lag = lax.axis_index("lag")
    block_size = inverse.shape[1]
    depth = capacity * block_size
    pieces = [len(own[step]) for step in range(steps)]

    def rows_of(step, piece):
        size = block_size // pieces[step]
        return pl.ds(piece * size, size)

    barrier = pltpu.get_barrier_semaphore()
    for away in range(1, rows):
        pl.semaphore_signal(barrier, inc=1, device_id=(lax.rem(row + away, rows), lag), device_id_type=MESH)
    for away in range(1, lags):
        pl.semaphore_signal(barrier, inc=1, device_id=(row, lax.rem(lag + away, lags)), device_id_type=MESH)

    own_table = pltpu.make_async_copy(table, asked_scalar.at[rows - 1], local_sem.at[0])
    own_table.start()

    def apply_inverse(block, value):
        return jnp.dot(
            inverse[block], value, precision=lax.Precision.HIGHEST, preferred_element_type=jnp.float32
        )

    def solved_part(step, before):
        parts = []
        for block in range(row_blocks):
            place = pl.ds(block * block_size, block_size)
            parts.append(apply_inverse(block, excitation[step, place].astype(jnp.float32) - before[place]))
        return jnp.concatenate(parts, axis=0)

    def keep_currents(step, value):
        value = value.astype(jnp.bfloat16).reshape(row_blocks, block_size, value.shape[-1])
        size = block_size // pieces[step]
        for piece in range(pieces[step]):
            own[step][piece][...] = value[:, piece * size : (piece + 1) * size]

    @pl.when(lag == 0)
    def _():
        keep_currents(0, solved_part(0, pending.at[0]))

    pl.semaphore_wait(barrier, rows + lags - 2)

    def ask_copy(away):
        target = lax.rem(row + away, rows)
        return pltpu.make_async_remote_copy(
            src_ref=table, dst_ref=asked.at[away - 1], send_sem=ask_send.at[away - 1],
            recv_sem=ask_recv.at[away - 1], device_id=(target, lag), device_id_type=MESH,
        )

    def row_copy(step, piece, away):
        target = lax.rem(row + away, rows)
        return pltpu.make_async_remote_copy(
            src_ref=sending.at[step, away - 1, :, rows_of(step, piece)],
            dst_ref=landed.at[step, away, :, rows_of(step, piece)],
            send_sem=row_send.at[step, piece, away - 1], recv_sem=row_recv.at[step, piece, away - 1],
            device_id=(target, lag), device_id_type=MESH,
        )

    def lag_copy(step, piece, target, which):
        return pltpu.make_async_remote_copy(
            src_ref=own[step][piece], dst_ref=own[step][piece],
            send_sem=lag_send.at[step, piece, which], recv_sem=lag_recv.at[step, piece],
            device_id=(row, target), device_id_type=MESH,
        )

    def hand_copy(step):
        source = pending.at[0] if step == 0 else summed.at[step - 1]
        return pltpu.make_async_remote_copy(
            src_ref=source, dst_ref=handed.at[step],
            send_sem=hand_send.at[step], recv_sem=hand_recv.at[step],
            device_id=(row, lax.rem(lag + lags - 1, lags)), device_id_type=MESH,
        )

    def out_copy(step, piece):
        return pltpu.make_async_copy(
            own[step][piece], currents.at[step, :, rows_of(step, piece)], out_sem.at[step, piece]
        )

    def product_of(step, away, first, second):
        place = pl.ds(away * depth, depth)
        values = landed[step, away].reshape(depth, landed.shape[-1])
        return jnp.dot(first[:, place], values, preferred_element_type=jnp.float32) + jnp.dot(
            second[:, place], values, preferred_element_type=jnp.float32
        )

    def product(step, first, second):
        total = product_of(step, 0, first, second)
        for away in range(1, rows):
            for piece in range(pieces[step]):
                row_copy(step, piece, away).wait_recv()
            total += product_of(step, away, first, second)
        return total

    for away in range(1, rows):
        ask_copy(away).start()

    @pl.when(lag > 0)
    def _():
        hand_copy(0).start()

    @pl.when(lag == lags - 1)
    def _():
        handed[...] = jnp.zeros_like(handed)

    to_scalar = pltpu.make_async_copy(asked, asked_scalar.at[pl.ds(0, rows - 1)], local_sem.at[1])
    evens = list(range(2, lags, 2))
    forwards = (lag > 0) & (lax.rem(lag, 2) == 0) & (lag + 1 < lags)

    def send_evens(step, piece):
        for place, target in enumerate(evens):
            lag_copy(step, piece, target, place + 1).start()

    for step in range(steps):
        last = step == steps - 1

        if last:
            @pl.when(lag == 0)
            def _():
                for piece in range(pieces[step]):
                    send_evens(step, piece)
                    lag_copy(step, piece, 1, 0).start()

        for piece in range(pieces[step]):
            @pl.when(lag > 0)
            def _():
                lag_copy(step, piece, 0, 0).wait_recv()

            if step == 0:
                for away in range(1, rows):
                    ask_copy(away).wait_recv()
                to_scalar.start()
                own_table.wait()
                to_scalar.wait()

            @pl.when(forwards)
            def _():
                lag_copy(step, piece, lag + 1, 0).start()

            place = rows_of(step, piece)
            for away in range(1, rows):
                for entry in range(capacity):
                    block = asked_scalar[rows - away - 1, row, entry]
                    sending[step, away - 1, entry, place] = own[step][piece][block]
            for away in range(1, rows):
                row_copy(step, piece, away).start()

            if not last:
                @pl.when(lag == 0)
                def _():
                    lag_copy(step, piece, 1, 0).start()
                    send_evens(step, piece)

            out_copy(step, piece).start()
            for entry in range(capacity):
                landed[step, 0, entry, place] = own[step][piece][asked_scalar[rows - 1, row, entry]]

        if last:
            total = product(step, high, low)

            @pl.when(lag < lags - 1)
            def _():
                hand_copy(step).wait_recv()

            carried[0] = handed[step] + total
            continue

        @pl.when(lag == 0)
        def _():
            if step == 0:
                for block in range(row_blocks):
                    place = pl.ds(block * block_size, block_size)
                    value = high[place].astype(jnp.float32) + low[place].astype(jnp.float32)
                    solve_high[place], solve_low[place] = split(apply_inverse(block, value))
            hand_copy(step).wait_recv()
            base = solved_part(step + 1, handed.at[step])
            keep_currents(step + 1, base - product(step, solve_high, solve_low))

        @pl.when(lag > 0)
        def _():
            total = product(step, high, low)

            @pl.when(lag < lags - 1)
            def _():
                hand_copy(step).wait_recv()

            summed[step] = handed[step] + total
            hand_copy(step + 1).start()

    for away in range(1, rows):
        ask_copy(away).wait_send()
    for step in range(steps):
        @pl.when(lag > 0)
        def _():
            hand_copy(step).wait_send()

        for piece in range(pieces[step]):
            def wait_rows():
                for away in range(1, rows):
                    row_copy(step, piece, away).wait_send()

            wait_rows()
            out_copy(step, piece).wait()

            @pl.when(forwards)
            def _():
                lag_copy(step, piece, lag + 1, 0).wait_send()

            @pl.when(lag == 0)
            def _():
                lag_copy(step, piece, 1, 0).wait_send()
                for place, target in enumerate(evens):
                    lag_copy(step, piece, target, place + 1).wait_send()


def per_device(
    excitation, pending, inverse, interaction, slot_row, slot_owner, slot_pos, needed, block_count
):
    row_blocks, block_size, _ = inverse.shape
    steps, unknowns, width = excitation.shape
    rows, capacity = needed.shape[1:]
    lags = lax.axis_size("lag")
    high, low = collapse(
        interaction, slot_row, slot_owner, slot_pos, block_count, row_blocks, rows, capacity
    )
    table = jnp.pad(needed[0], ((0, -rows % 8), (0, -capacity % 128)))
    vmem = pl.BlockSpec(memory_space=pltpu.VMEM)
    dma = pltpu.SemaphoreType.DMA
    evens = len(range(2, lags, 2))
    tail = 2 if block_size % 32 == 0 else 1
    return pl.pallas_call(
        functools.partial(window_kernel, rows, lags, steps, row_blocks, capacity),
        out_shape=[
            jax.ShapeDtypeStruct((steps, row_blocks, block_size, width), jnp.bfloat16),
            jax.ShapeDtypeStruct((1, unknowns, width), jnp.float32),
        ],
        in_specs=[vmem] * 6,
        out_specs=[vmem, vmem],
        scratch_shapes=[
            pltpu.VMEM(high.shape, jnp.bfloat16),
            pltpu.VMEM(low.shape, jnp.bfloat16),
            [
                [pltpu.VMEM((row_blocks, block_size // cut, width), jnp.bfloat16)] * cut
                for cut in [1] * (steps - 1) + [tail]
            ],
            pltpu.VMEM((steps, rows - 1, capacity, block_size, width), jnp.bfloat16),
            pltpu.VMEM((steps, rows, capacity, block_size, width), jnp.bfloat16),
            pltpu.VMEM((steps, unknowns, width), jnp.float32),
            pltpu.VMEM((steps, unknowns, width), jnp.float32),
            pltpu.VMEM((rows - 1,) + table.shape, jnp.int32),
            pltpu.SMEM((rows,) + table.shape, jnp.int32),
            dma((steps, tail, rows - 1)),
            dma((steps, tail, rows - 1)),
            dma((steps, tail, evens + 1)),
            dma((steps, tail)),
            dma((steps,)),
            dma((steps,)),
            dma((rows - 1,)),
            dma((rows - 1,)),
            dma((2,)),
            dma((steps, tail)),
        ],
        compiler_params=pltpu.CompilerParams(
            collective_id=0, has_side_effects=True, vmem_limit_bytes=48 * 1024 * 1024
        ),
    )(excitation, pending, inverse, table, high, low)


def solution(mesh):
    in_specs = (
        P(None, "rows", None),
        P("lag", "rows", None),
        P("rows", None, None),
        P(("rows", "lag"), None, None),
        P(("rows", "lag")),
        P(("rows", "lag")),
        P(("rows", "lag")),
        P(("rows", "lag"), None, None),
        P("rows", "lag"),
    )
    out_specs = (P(None, "rows", None), P("lag", "rows", None))

    def body(*arrays):
        currents, carried = per_device(*arrays)
        return currents.reshape(arrays[0].shape), carried

    return jax.shard_map(body, mesh=mesh, in_specs=in_specs, out_specs=out_specs, check_vma=False)
```

```python
import functools

import jax
import jax.numpy as jnp
from jax import lax
from jax.experimental import pallas as pl
from jax.experimental.pallas import tpu as pltpu
from jax.sharding import PartitionSpec as P

MESH = pl.DeviceIdType.MESH


def split(value):
    high = value.astype(jnp.bfloat16)
    return high, (value - high.astype(jnp.float32)).astype(jnp.bfloat16)


def collapse_kernel(chunk, cell_ref, block_hbm, high_ref, low_ref, blocks, total, sems):
    columns, block_size = total.shape[1] // total.shape[2], total.shape[2]
    cells = total.shape[0] * columns
    slots = blocks.shape[0]

    def fetch(part):
        place = pl.ds(part * chunk, chunk)
        return pltpu.make_async_copy(block_hbm.at[place], blocks.at[place], sems.at[part])

    for part in range(slots // chunk):
        fetch(part).start()
    total[...] = jnp.zeros_like(total)
    live = cell_ref[slots]

    def add_slot(slot, carry):
        cell = cell_ref[slot]
        row = lax.div(cell, columns)
        start = pl.multiple_of(lax.rem(cell, columns) * block_size, block_size)
        total[row, pl.ds(start, block_size)] += blocks[slot].astype(jnp.float32)
        return carry

    for part in range(slots // chunk):
        fetch(part).wait()
        lax.fori_loop(part * chunk, jnp.clip(live, part * chunk, (part + 1) * chunk), add_slot, 0)

    for cell in range(cells):
        row, column = divmod(cell, columns)
        place = (pl.ds(row * block_size, block_size), pl.ds(column * block_size, block_size))
        high_ref[place], low_ref[place] = split(total[row, pl.ds(column * block_size, block_size)])


def collapse(interaction, slot_row, slot_owner, slot_pos, block_count, row_blocks, rows, capacity):
    slots, block_size, _ = interaction.shape
    columns = rows * capacity
    chunk = max(size for size in range(1, 17) if slots % size == 0)
    away = lax.rem(lax.axis_index("rows") + rows - slot_owner, rows)
    cell = slot_row * columns + away * capacity + slot_pos
    cell = jnp.concatenate([cell, block_count[0]])
    shape = (row_blocks * block_size, columns * block_size)
    vmem = pl.BlockSpec(memory_space=pltpu.VMEM)
    return pl.pallas_call(
        functools.partial(collapse_kernel, chunk),
        in_specs=[pl.BlockSpec(memory_space=pltpu.SMEM), pl.BlockSpec(memory_space=pltpu.HBM)],
        out_specs=[vmem, vmem],
        scratch_shapes=[
            pltpu.VMEM(interaction.shape, jnp.bfloat16),
            pltpu.VMEM((row_blocks, columns * block_size, block_size), jnp.float32),
            pltpu.SemaphoreType.DMA((slots // chunk,)),
        ],
        out_shape=[jax.ShapeDtypeStruct(shape, jnp.bfloat16)] * 2,
        compiler_params=pltpu.CompilerParams(vmem_limit_bytes=50 * 1024 * 1024),
    )(cell, interaction)


def window_kernel(
    rows, lags, steps, row_blocks, capacity,
    excitation, pending, inverse, table, high, low,
    currents, carried,
    solve_high, solve_low, own, sending, landed, handed, summed, asked, asked_scalar,
    row_send, row_recv, lag_send, lag_recv, hand_send, hand_recv, ask_send, ask_recv, local_sem, out_sem,
):
    row = lax.axis_index("rows")
    lag = lax.axis_index("lag")
    block_size = inverse.shape[1]
    depth = capacity * block_size
    pieces = [len(own[step]) for step in range(steps)]

    def rows_of(step, piece):
        size = block_size // pieces[step]
        return pl.ds(piece * size, size)

    barrier = pltpu.get_barrier_semaphore()
    for away in range(1, rows):
        pl.semaphore_signal(barrier, inc=1, device_id=(lax.rem(row + away, rows), lag), device_id_type=MESH)
    for away in range(1, lags):
        pl.semaphore_signal(barrier, inc=1, device_id=(row, lax.rem(lag + away, lags)), device_id_type=MESH)

    own_table = pltpu.make_async_copy(table, asked_scalar.at[rows - 1], local_sem.at[0])
    own_table.start()

    def apply_inverse(block, value):
        return jnp.dot(
            inverse[block], value, precision=lax.Precision.HIGHEST, preferred_element_type=jnp.float32
        )

    def solved_part(step, before):
        parts = []
        for block in range(row_blocks):
            place = pl.ds(block * block_size, block_size)
            parts.append(apply_inverse(block, excitation[step, place].astype(jnp.float32) - before[place]))
        return jnp.concatenate(parts, axis=0)

    def keep_currents(step, value):
        value = value.astype(jnp.bfloat16).reshape(row_blocks, block_size, value.shape[-1])
        size = block_size // pieces[step]
        for piece in range(pieces[step]):
            own[step][piece][...] = value[:, piece * size : (piece + 1) * size]

    @pl.when(lag == 0)
    def _():
        keep_currents(0, solved_part(0, pending.at[0]))

    pl.semaphore_wait(barrier, rows + lags - 2)

    def ask_copy(away):
        target = lax.rem(row + away, rows)
        return pltpu.make_async_remote_copy(
            src_ref=table, dst_ref=asked.at[away - 1], send_sem=ask_send.at[away - 1],
            recv_sem=ask_recv.at[away - 1], device_id=(target, lag), device_id_type=MESH,
        )

    def row_copy(step, piece, away):
        target = lax.rem(row + away, rows)
        return pltpu.make_async_remote_copy(
            src_ref=sending.at[step, away - 1, :, rows_of(step, piece)],
            dst_ref=landed.at[step, away, :, rows_of(step, piece)],
            send_sem=row_send.at[step, piece, away - 1], recv_sem=row_recv.at[step, piece, away - 1],
            device_id=(target, lag), device_id_type=MESH,
        )

    def lag_copy(step, piece, target, which):
        return pltpu.make_async_remote_copy(
            src_ref=own[step][piece], dst_ref=own[step][piece],
            send_sem=lag_send.at[step, piece, which], recv_sem=lag_recv.at[step, piece],
            device_id=(row, target), device_id_type=MESH,
        )

    def hand_copy(step):
        source = pending.at[0] if step == 0 else summed.at[step - 1]
        return pltpu.make_async_remote_copy(
            src_ref=source, dst_ref=handed.at[step],
            send_sem=hand_send.at[step], recv_sem=hand_recv.at[step],
            device_id=(row, lax.rem(lag + lags - 1, lags)), device_id_type=MESH,
        )

    def out_copy(step, piece):
        return pltpu.make_async_copy(
            own[step][piece], currents.at[step, :, rows_of(step, piece)], out_sem.at[step, piece]
        )

    def product_of(step, away, first, second):
        place = pl.ds(away * depth, depth)
        values = landed[step, away].reshape(depth, landed.shape[-1])
        return jnp.dot(first[:, place], values, preferred_element_type=jnp.float32) + jnp.dot(
            second[:, place], values, preferred_element_type=jnp.float32
        )

    def product(step, first, second):
        total = product_of(step, 0, first, second)
        for away in range(1, rows):
            for piece in range(pieces[step]):
                row_copy(step, piece, away).wait_recv()
            total += product_of(step, away, first, second)
        return total

    for away in range(1, rows):
        ask_copy(away).start()

    @pl.when(lag > 0)
    def _():
        hand_copy(0).start()

    @pl.when(lag == lags - 1)
    def _():
        handed[...] = jnp.zeros_like(handed)

    to_scalar = pltpu.make_async_copy(asked, asked_scalar.at[pl.ds(0, rows - 1)], local_sem.at[1])
    evens = list(range(2, lags, 2))
    forwards = (lag > 0) & (lax.rem(lag, 2) == 0) & (lag + 1 < lags)

    def send_evens(step, piece):
        for place, target in reversed(list(enumerate(evens))):
            lag_copy(step, piece, target, place + 1).start()

    for step in range(steps):
        last = step == steps - 1

        if last:
            @pl.when(lag == 0)
            def _():
                for piece in range(pieces[step]):
                    send_evens(step, piece)
                    lag_copy(step, piece, 1, 0).start()

        for piece in range(pieces[step]):
            @pl.when(lag > 0)
            def _():
                lag_copy(step, piece, 0, 0).wait_recv()

            if step == 0:
                for away in range(1, rows):
                    ask_copy(away).wait_recv()
                to_scalar.start()
                own_table.wait()
                to_scalar.wait()

            @pl.when(forwards)
            def _():
                lag_copy(step, piece, lag + 1, 0).start()

            place = rows_of(step, piece)
            for away in range(1, rows):
                for entry in range(capacity):
                    block = asked_scalar[rows - away - 1, row, entry]
                    sending[step, away - 1, entry, place] = own[step][piece][block]
            for away in range(1, rows):
                row_copy(step, piece, away).start()

            if not last:
                @pl.when(lag == 0)
                def _():
                    lag_copy(step, piece, 1, 0).start()
                    send_evens(step, piece)

            out_copy(step, piece).start()
            for entry in range(capacity):
                landed[step, 0, entry, place] = own[step][piece][asked_scalar[rows - 1, row, entry]]

        if last:
            total = product(step, high, low)

            @pl.when(lag < lags - 1)
            def _():
                hand_copy(step).wait_recv()

            carried[0] = handed[step] + total
            continue

        @pl.when(lag == 0)
        def _():
            if step == 0:
                for block in range(row_blocks):
                    place = pl.ds(block * block_size, block_size)
                    value = high[place].astype(jnp.float32) + low[place].astype(jnp.float32)
                    solve_high[place], solve_low[place] = split(apply_inverse(block, value))
            hand_copy(step).wait_recv()
            base = solved_part(step + 1, handed.at[step])
            keep_currents(step + 1, base - product(step, solve_high, solve_low))

        @pl.when(lag > 0)
        def _():
            total = product(step, high, low)

            @pl.when(lag < lags - 1)
            def _():
                hand_copy(step).wait_recv()

            summed[step] = handed[step] + total
            hand_copy(step + 1).start()

    for away in range(1, rows):
        ask_copy(away).wait_send()
    for step in range(steps):
        @pl.when(lag > 0)
        def _():
            hand_copy(step).wait_send()

        for piece in range(pieces[step]):
            def wait_rows():
                for away in range(1, rows):
                    row_copy(step, piece, away).wait_send()

            wait_rows()
            out_copy(step, piece).wait()

            @pl.when(forwards)
            def _():
                lag_copy(step, piece, lag + 1, 0).wait_send()

            @pl.when(lag == 0)
            def _():
                lag_copy(step, piece, 1, 0).wait_send()
                for place, target in enumerate(evens):
                    lag_copy(step, piece, target, place + 1).wait_send()


def per_device(
    excitation, pending, inverse, interaction, slot_row, slot_owner, slot_pos, needed, block_count
):
    row_blocks, block_size, _ = inverse.shape
    steps, unknowns, width = excitation.shape
    rows, capacity = needed.shape[1:]
    lags = lax.axis_size("lag")
    high, low = collapse(
        interaction, slot_row, slot_owner, slot_pos, block_count, row_blocks, rows, capacity
    )
    lanes = jnp.arange(capacity + -capacity % 128, dtype=jnp.int32)[None, None, :]
    spread = sum(jnp.where(lanes == entry, needed[:, :, entry : entry + 1], 0) for entry in range(capacity))
    table = jnp.pad(spread, ((0, 0), (0, -rows % 8), (0, 0)))[0]
    vmem = pl.BlockSpec(memory_space=pltpu.VMEM)
    dma = pltpu.SemaphoreType.DMA
    evens = len(range(2, lags, 2))
    tail = 4 if block_size % 64 == 0 else 1
    return pl.pallas_call(
        functools.partial(window_kernel, rows, lags, steps, row_blocks, capacity),
        out_shape=[
            jax.ShapeDtypeStruct((steps, row_blocks, block_size, width), jnp.bfloat16),
            jax.ShapeDtypeStruct((1, unknowns, width), jnp.float32),
        ],
        in_specs=[vmem] * 6,
        out_specs=[vmem, vmem],
        scratch_shapes=[
            pltpu.VMEM(high.shape, jnp.bfloat16),
            pltpu.VMEM(low.shape, jnp.bfloat16),
            [
                [pltpu.VMEM((row_blocks, block_size // cut, width), jnp.bfloat16)] * cut
                for cut in [1] * (steps - 1) + [tail]
            ],
            pltpu.VMEM((steps, rows - 1, capacity, block_size, width), jnp.bfloat16),
            pltpu.VMEM((steps, rows, capacity, block_size, width), jnp.bfloat16),
            pltpu.VMEM((steps, unknowns, width), jnp.float32),
            pltpu.VMEM((steps, unknowns, width), jnp.float32),
            pltpu.VMEM((rows - 1,) + table.shape, jnp.int32),
            pltpu.SMEM((rows,) + table.shape, jnp.int32),
            dma((steps, tail, rows - 1)),
            dma((steps, tail, rows - 1)),
            dma((steps, tail, evens + 1)),
            dma((steps, tail)),
            dma((steps,)),
            dma((steps,)),
            dma((rows - 1,)),
            dma((rows - 1,)),
            dma((2,)),
            dma((steps, tail)),
        ],
        compiler_params=pltpu.CompilerParams(
            collective_id=0, has_side_effects=True, vmem_limit_bytes=48 * 1024 * 1024
        ),
    )(excitation, pending, inverse, table, high, low)


def solution(mesh):
    in_specs = (
        P(None, "rows", None),
        P("lag", "rows", None),
        P("rows", None, None),
        P(("rows", "lag"), None, None),
        P(("rows", "lag")),
        P(("rows", "lag")),
        P(("rows", "lag")),
        P(("rows", "lag"), None, None),
        P("rows", "lag"),
    )
    out_specs = (P(None, "rows", None), P("lag", "rows", None))

    def body(*arrays):
        currents, carried = per_device(*arrays)
        return currents.reshape(arrays[0].shape), carried

    return jax.shard_map(body, mesh=mesh, in_specs=in_specs, out_specs=out_specs, check_vma=False)
```

```python
import functools

import jax
import jax.numpy as jnp
from jax import lax
from jax.experimental import pallas as pl
from jax.experimental.pallas import tpu as pltpu
from jax.sharding import PartitionSpec as P

MESH = pl.DeviceIdType.MESH


def split(value):
    high = value.astype(jnp.bfloat16)
    return high, (value - high.astype(jnp.float32)).astype(jnp.bfloat16)


def collapse_kernel(chunk, cell_ref, block_hbm, high_ref, low_ref, blocks, total, sems):
    columns, block_size = total.shape[1] // total.shape[2], total.shape[2]
    cells = total.shape[0] * columns
    slots = blocks.shape[0]

    def fetch(part):
        place = pl.ds(part * chunk, chunk)
        return pltpu.make_async_copy(block_hbm.at[place], blocks.at[place], sems.at[part])

    for part in range(slots // chunk):
        fetch(part).start()
    total[...] = jnp.zeros_like(total)
    live = cell_ref[slots]

    def add_slot(slot, carry):
        cell = cell_ref[slot]
        row = lax.div(cell, columns)
        start = pl.multiple_of(lax.rem(cell, columns) * block_size, block_size)
        total[row, pl.ds(start, block_size)] += blocks[slot].astype(jnp.float32)
        return carry

    for part in range(slots // chunk):
        fetch(part).wait()
        lax.fori_loop(part * chunk, jnp.clip(live, part * chunk, (part + 1) * chunk), add_slot, 0)

    for cell in range(cells):
        row, column = divmod(cell, columns)
        place = (pl.ds(row * block_size, block_size), pl.ds(column * block_size, block_size))
        high_ref[place], low_ref[place] = split(total[row, pl.ds(column * block_size, block_size)])


def collapse(interaction, slot_row, slot_owner, slot_pos, block_count, row_blocks, rows, capacity):
    slots, block_size, _ = interaction.shape
    columns = rows * capacity
    chunk = max(size for size in range(1, 17) if slots % size == 0)
    away = lax.rem(lax.axis_index("rows") + rows - slot_owner, rows)
    cell = slot_row * columns + away * capacity + slot_pos
    cell = jnp.concatenate([cell, block_count[0]])
    shape = (row_blocks * block_size, columns * block_size)
    vmem = pl.BlockSpec(memory_space=pltpu.VMEM)
    return pl.pallas_call(
        functools.partial(collapse_kernel, chunk),
        in_specs=[pl.BlockSpec(memory_space=pltpu.SMEM), pl.BlockSpec(memory_space=pltpu.HBM)],
        out_specs=[vmem, vmem],
        scratch_shapes=[
            pltpu.VMEM(interaction.shape, jnp.bfloat16),
            pltpu.VMEM((row_blocks, columns * block_size, block_size), jnp.float32),
            pltpu.SemaphoreType.DMA((slots // chunk,)),
        ],
        out_shape=[jax.ShapeDtypeStruct(shape, jnp.bfloat16)] * 2,
        compiler_params=pltpu.CompilerParams(vmem_limit_bytes=50 * 1024 * 1024),
    )(cell, interaction)


def window_kernel(
    rows, lags, steps, row_blocks, capacity,
    excitation, pending, inverse, table, high, low,
    currents, carried,
    solve_high, solve_low, own, sending, landed, handed, summed, asked, asked_scalar,
    row_send, row_recv, lag_send, lag_recv, hand_send, hand_recv, ask_send, ask_recv, local_sem, out_sem,
):
    row = lax.axis_index("rows")
    lag = lax.axis_index("lag")
    block_size = inverse.shape[1]
    depth = capacity * block_size
    pieces = [len(own[step]) for step in range(steps)]

    def rows_of(step, piece):
        size = block_size // pieces[step]
        return pl.ds(piece * size, size)

    barrier = pltpu.get_barrier_semaphore()
    for away in range(1, rows):
        pl.semaphore_signal(barrier, inc=1, device_id=(lax.rem(row + away, rows), lag), device_id_type=MESH)
    for away in range(1, lags):
        pl.semaphore_signal(barrier, inc=1, device_id=(row, lax.rem(lag + away, lags)), device_id_type=MESH)

    own_table = pltpu.make_async_copy(table, asked_scalar.at[rows - 1], local_sem.at[0])
    own_table.start()

    def apply_inverse(block, value):
        return jnp.dot(
            inverse[block], value, precision=lax.Precision.HIGHEST, preferred_element_type=jnp.float32
        )

    def solved_part(step, before):
        parts = []
        for block in range(row_blocks):
            place = pl.ds(block * block_size, block_size)
            parts.append(apply_inverse(block, excitation[step, place].astype(jnp.float32) - before[place]))
        return jnp.concatenate(parts, axis=0)

    def keep_currents(step, value):
        value = value.astype(jnp.bfloat16).reshape(row_blocks, block_size, value.shape[-1])
        size = block_size // pieces[step]
        for piece in range(pieces[step]):
            own[step][piece][...] = value[:, piece * size : (piece + 1) * size]

    @pl.when(lag == 0)
    def _():
        keep_currents(0, solved_part(0, pending.at[0]))

    pl.semaphore_wait(barrier, rows + lags - 2)

    def ask_copy(away):
        target = lax.rem(row + away, rows)
        return pltpu.make_async_remote_copy(
            src_ref=table, dst_ref=asked.at[away - 1], send_sem=ask_send.at[away - 1],
            recv_sem=ask_recv.at[away - 1], device_id=(target, lag), device_id_type=MESH,
        )

    def row_copy(step, piece, away):
        target = lax.rem(row + away, rows)
        return pltpu.make_async_remote_copy(
            src_ref=sending.at[step, away - 1, :, rows_of(step, piece)],
            dst_ref=landed.at[step, away, :, rows_of(step, piece)],
            send_sem=row_send.at[step, piece, away - 1], recv_sem=row_recv.at[step, piece, away - 1],
            device_id=(target, lag), device_id_type=MESH,
        )

    def lag_copy(step, piece, target, which):
        return pltpu.make_async_remote_copy(
            src_ref=own[step][piece], dst_ref=own[step][piece],
            send_sem=lag_send.at[step, piece, which], recv_sem=lag_recv.at[step, piece],
            device_id=(row, target), device_id_type=MESH,
        )

    def hand_copy(step):
        source = pending.at[0] if step == 0 else summed.at[step - 1]
        return pltpu.make_async_remote_copy(
            src_ref=source, dst_ref=handed.at[step],
            send_sem=hand_send.at[step], recv_sem=hand_recv.at[step],
            device_id=(row, lax.rem(lag + lags - 1, lags)), device_id_type=MESH,
        )

    def out_copy(step, piece):
        return pltpu.make_async_copy(
            own[step][piece], currents.at[step, :, rows_of(step, piece)], out_sem.at[step, piece]
        )

    def product_of(step, away, first, second):
        place = pl.ds(away * depth, depth)
        values = landed[step, away].reshape(depth, landed.shape[-1])
        return jnp.dot(first[:, place], values, preferred_element_type=jnp.float32) + jnp.dot(
            second[:, place], values, preferred_element_type=jnp.float32
        )

    def product(step, first, second):
        total = product_of(step, 0, first, second)
        for away in range(1, rows):
            for piece in range(pieces[step]):
                row_copy(step, piece, away).wait_recv()
            total += product_of(step, away, first, second)
        return total

    for away in range(1, rows):
        ask_copy(away).start()

    @pl.when(lag > 0)
    def _():
        hand_copy(0).start()

    @pl.when(lag == lags - 1)
    def _():
        handed[...] = jnp.zeros_like(handed)

    to_scalar = pltpu.make_async_copy(asked, asked_scalar.at[pl.ds(0, rows - 1)], local_sem.at[1])
    evens = [target for target in range(2, lags, 2) if target == 2 or target % 4 == 0]
    relays = (lag > 0) & (lax.rem(lag, 4) == 0) & (lag + 2 < lags)
    forwards = (lag > 0) & (lax.rem(lag, 2) == 0) & (lag + 1 < lags)

    def send_evens(step, piece):
        for place, target in enumerate(evens):
            lag_copy(step, piece, target, place + 1).start()

    for step in range(steps):
        last = step == steps - 1

        if last:
            @pl.when(lag == 0)
            def _():
                for piece in range(pieces[step]):
                    send_evens(step, piece)
                    lag_copy(step, piece, 1, 0).start()

        for piece in range(pieces[step]):
            @pl.when(lag > 0)
            def _():
                lag_copy(step, piece, 0, 0).wait_recv()

            if step == 0:
                for away in range(1, rows):
                    ask_copy(away).wait_recv()
                to_scalar.start()
                own_table.wait()
                to_scalar.wait()

            @pl.when(relays)
            def _():
                lag_copy(step, piece, lag + 2, 1).start()

            @pl.when(forwards)
            def _():
                lag_copy(step, piece, lag + 1, 0).start()

            place = rows_of(step, piece)
            for away in range(1, rows):
                for entry in range(capacity):
                    block = asked_scalar[rows - away - 1, row, entry]
                    sending[step, away - 1, entry, place] = own[step][piece][block]
            for away in range(1, rows):
                row_copy(step, piece, away).start()

            if not last:
                @pl.when(lag == 0)
                def _():
                    lag_copy(step, piece, 1, 0).start()
                    send_evens(step, piece)

            out_copy(step, piece).start()
            for entry in range(capacity):
                landed[step, 0, entry, place] = own[step][piece][asked_scalar[rows - 1, row, entry]]

        if last:
            total = product(step, high, low)

            @pl.when(lag < lags - 1)
            def _():
                hand_copy(step).wait_recv()

            carried[0] = handed[step] + total
            continue

        @pl.when(lag == 0)
        def _():
            if step == 0:
                for block in range(row_blocks):
                    place = pl.ds(block * block_size, block_size)
                    value = high[place].astype(jnp.float32) + low[place].astype(jnp.float32)
                    solve_high[place], solve_low[place] = split(apply_inverse(block, value))
            hand_copy(step).wait_recv()
            base = solved_part(step + 1, handed.at[step])
            keep_currents(step + 1, base - product(step, solve_high, solve_low))

        @pl.when(lag > 0)
        def _():
            total = product(step, high, low)

            @pl.when(lag < lags - 1)
            def _():
                hand_copy(step).wait_recv()

            summed[step] = handed[step] + total
            hand_copy(step + 1).start()

    for away in range(1, rows):
        ask_copy(away).wait_send()
    for step in range(steps):
        @pl.when(lag > 0)
        def _():
            hand_copy(step).wait_send()

        for piece in range(pieces[step]):
            def wait_rows():
                for away in range(1, rows):
                    row_copy(step, piece, away).wait_send()

            wait_rows()
            out_copy(step, piece).wait()

            @pl.when(relays)
            def _():
                lag_copy(step, piece, lag + 2, 1).wait_send()

            @pl.when(forwards)
            def _():
                lag_copy(step, piece, lag + 1, 0).wait_send()

            @pl.when(lag == 0)
            def _():
                lag_copy(step, piece, 1, 0).wait_send()
                for place, target in enumerate(evens):
                    lag_copy(step, piece, target, place + 1).wait_send()


def per_device(
    excitation, pending, inverse, interaction, slot_row, slot_owner, slot_pos, needed, block_count
):
    row_blocks, block_size, _ = inverse.shape
    steps, unknowns, width = excitation.shape
    rows, capacity = needed.shape[1:]
    lags = lax.axis_size("lag")
    high, low = collapse(
        interaction, slot_row, slot_owner, slot_pos, block_count, row_blocks, rows, capacity
    )
    table = jnp.pad(needed[0], ((0, -rows % 8), (0, -capacity % 128)))
    vmem = pl.BlockSpec(memory_space=pltpu.VMEM)
    dma = pltpu.SemaphoreType.DMA
    evens = len(range(2, lags, 2))
    tail = 2 if block_size % 32 == 0 else 1
    return pl.pallas_call(
        functools.partial(window_kernel, rows, lags, steps, row_blocks, capacity),
        out_shape=[
            jax.ShapeDtypeStruct((steps, row_blocks, block_size, width), jnp.bfloat16),
            jax.ShapeDtypeStruct((1, unknowns, width), jnp.float32),
        ],
        in_specs=[vmem] * 6,
        out_specs=[vmem, vmem],
        scratch_shapes=[
            pltpu.VMEM(high.shape, jnp.bfloat16),
            pltpu.VMEM(low.shape, jnp.bfloat16),
            [
                [pltpu.VMEM((row_blocks, block_size // cut, width), jnp.bfloat16)] * cut
                for cut in [1] * (steps - 1) + [tail]
            ],
            pltpu.VMEM((steps, rows - 1, capacity, block_size, width), jnp.bfloat16),
            pltpu.VMEM((steps, rows, capacity, block_size, width), jnp.bfloat16),
            pltpu.VMEM((steps, unknowns, width), jnp.float32),
            pltpu.VMEM((steps, unknowns, width), jnp.float32),
            pltpu.VMEM((rows - 1,) + table.shape, jnp.int32),
            pltpu.SMEM((rows,) + table.shape, jnp.int32),
            dma((steps, tail, rows - 1)),
            dma((steps, tail, rows - 1)),
            dma((steps, tail, evens + 1)),
            dma((steps, tail)),
            dma((steps,)),
            dma((steps,)),
            dma((rows - 1,)),
            dma((rows - 1,)),
            dma((2,)),
            dma((steps, tail)),
        ],
        compiler_params=pltpu.CompilerParams(
            collective_id=0, has_side_effects=True, vmem_limit_bytes=48 * 1024 * 1024
        ),
    )(excitation, pending, inverse, table, high, low)


def solution(mesh):
    in_specs = (
        P(None, "rows", None),
        P("lag", "rows", None),
        P("rows", None, None),
        P(("rows", "lag"), None, None),
        P(("rows", "lag")),
        P(("rows", "lag")),
        P(("rows", "lag")),
        P(("rows", "lag"), None, None),
        P("rows", "lag"),
    )
    out_specs = (P(None, "rows", None), P("lag", "rows", None))

    def body(*arrays):
        currents, carried = per_device(*arrays)
        return currents.reshape(arrays[0].shape), carried

    return jax.shard_map(body, mesh=mesh, in_specs=in_specs, out_specs=out_specs, check_vma=False)
```
